32 devices in a mesh: dp: 16 (over z, y, x), sub: 2 (over core).
Axes of the slice: x: 2, y: 2, z: 4, core: 2. Of those that a mesh axis runs over, the one named last changes fastest.
Arguments:
- tokens: bfloat16 [128, 2048, 768], P(('dp', 'sub')), may hold values from -6 to 6
- doc_lengths: int32 [128, 16], P(('dp', 'sub')), may hold values from 1 to 2033, as said below
- selected: int32 [128, 256], P(('dp', 'sub')), may hold values from 0 to 2047, as said below
- w_router: bfloat16 [768], replicated, may hold values from -0.21875 to 0.21875
- gain_attn: bfloat16 [768], replicated, may hold values from 0.099609375 to 1.8984375
- w_qkv: bfloat16 [768, 2304], replicated, may hold values from -0.21875 to 0.21875
- w_out: bfloat16 [768, 768], replicated, may hold values from -0.875 to 0.875
- gain_mlp: bfloat16 [768], replicated, may hold values from 0.099609375 to 1.8984375
- w_up: bfloat16 [768, 3072], replicated, may hold values from -0.21875 to 0.21875
- b_up: bfloat16 [3072], replicated, may hold values from -3 to 3
- w_down: bfloat16 [3072, 768], replicated, may hold values from -0.109375 to 0.109375
- b_down: bfloat16 [768], replicated, may hold values from -3 to 3
- cotangent: bfloat16 [128, 2048, 768], P(('dp', 'sub')), may hold values from -6 to 6
Outputs:
- block_out: bfloat16 [128, 2048, 768], P(('dp', 'sub'))
- grad_tokens: bfloat16 [128, 2048, 768], P(('dp', 'sub'))
- grad_router: float32 [768], replicated
- grad_gain_attn: float32 [768], replicated
- grad_qkv: float32 [768, 2304], replicated
- grad_out: float32 [768, 768], replicated
- grad_gain_mlp: float32 [768], replicated
- grad_up: float32 [768, 3072], replicated
- grad_b_up: float32 [3072], replicated
- grad_down: float32 [3072, 768], replicated
- grad_b_down: float32 [768], replicated
The draws below stay inside these ranges and needn't reach their ends.
Inputs may be any that keep to these rules, and one draw needn't show every extreme that they name: `doc_lengths`: each row's lengths are positive and add up to at most 2048; positions past their sum are padding. `selected`: each row's positions are distinct and ascending.
All inputs are finite; a program needn't handle non-finite values.
Results may differ from the reference program's by a relative error of at most 0.0093.
Values sent between devices are 32-bit elements; how exact they have to be, the bound alone decides.
A program may use at most 256 MiB of HBM per device.

```python
import jax
import jax.numpy as jnp
from jax import lax

D = 768
HEADS = 12
HEAD = 64
FF = 3072
ROW_LEN = 2048
SEL = 256
DOCS = 16
ROWS = 128


def draw_doc_lengths(key, part):
    key = jax.random.fold_in(key, 11)
    share_key, slot_key = jax.random.split(key)
    row_index = jnp.arange(ROWS, dtype=jnp.int32)
    padding = 2 * ROW_LEN // 3 * (ROWS - 1 - row_index) // max(ROWS - 1, 1)
    valid = ROW_LEN - padding
    base = jax.random.randint(share_key, (ROWS, DOCS), 1, 41, dtype=jnp.int32)
    shares = base * base * base
    spare = valid - DOCS
    lengths = 1 + spare[:, None] * shares // jnp.sum(shares, axis=1, keepdims=True)
    missing = valid - jnp.sum(lengths, axis=1)
    last_slot = (jnp.arange(DOCS) == DOCS - 1).astype(jnp.int32)
    lengths = lengths + missing[:, None] * last_slot[None, :]
    big_slot = jax.random.randint(slot_key, (), 0, DOCS, dtype=jnp.int32)
    big_row = 1 + (ROW_LEN - DOCS) * (jnp.arange(DOCS, dtype=jnp.int32) == big_slot).astype(jnp.int32)
    is_last = (row_index == ROWS - 1)[:, None]
    return jnp.where(is_last, big_row[None, :], lengths)


def draw_selected(key, part):
    key = jax.random.fold_in(key, 12)
    row_keys = jax.random.split(key, ROWS)
    shuffled = jax.vmap(lambda single: jax.random.permutation(single, ROW_LEN))(row_keys)
    return jnp.sort(shuffled[:, :SEL].astype(jnp.int32), axis=1)


def shard_levels(key, extent, pieces, low, high):
    factor_of = 1.0
    for axis_at, shards_of in pieces:
        steps = jax.random.uniform(jax.random.fold_in(jax.random.fold_in(key, 6), axis_at), (shards_of,), jnp.float32, low / len(pieces), high / len(pieces))
        factor_of = factor_of * jnp.repeat(jnp.exp(steps), extent[axis_at] // shards_of).reshape((-1,) + (1,) * (len(extent) - 1 - axis_at))
    return factor_of


def centred(own_key, dims, scale, most, pieces=(), kind=jnp.bfloat16):
    values = scale * jax.random.normal(own_key, dims, jnp.float32)
    if pieces:
        values = values * shard_levels(own_key, dims, pieces, -0.22, 0.18)
    return jnp.clip(values, -most, most).astype(kind)


def setup_inputs(seed: int = 0) -> dict:
    streams_of = jax.random.split(jax.random.key(seed), 14)
    return {
        "tokens": centred(streams_of[0], (ROWS, ROW_LEN, D), 1.0, 6.0, ((0, 32),)),
        "doc_lengths": draw_doc_lengths(jax.random.fold_in(streams_of[13], 71), 0),
        "selected": draw_selected(jax.random.fold_in(streams_of[13], 71), 0),
        "w_router": centred(streams_of[3], (D,), D ** -0.5, 0.21875),
        "gain_attn": jnp.clip(1.0 + 0.18 * jax.random.normal(streams_of[4], (D,), jnp.float32), 0.099609375, 1.8984375).astype(jnp.bfloat16),
        "w_qkv": centred(streams_of[5], (D, 3 * D), D ** -0.5, 0.21875),
        "w_out": centred(streams_of[6], (D, D), (D // 16) ** -0.5, 0.875),
        "gain_mlp": jnp.clip(1.0 + 0.18 * jax.random.normal(streams_of[7], (D,), jnp.float32), 0.099609375, 1.8984375).astype(jnp.bfloat16),
        "w_up": centred(streams_of[8], (D, FF), D ** -0.5, 0.21875),
        "b_up": centred(streams_of[9], (FF,), 0.5, 3.0),
        "w_down": centred(streams_of[10], (FF, D), FF ** -0.5, 0.109375),
        "b_down": centred(streams_of[11], (D,), 0.5, 3.0),
        "cotangent": centred(streams_of[12], (ROWS, ROW_LEN, D), 1.0, 6.0, ((0, 32),)),
    }


@jax.custom_vjp
def low(v):
    return lax.optimization_barrier(v.astype(jnp.bfloat16)).astype(jnp.float32)

@jax.custom_vjp
def low_back(v):
    return v

def low_keep(v):
    return (low(v), None)

def low_pass(kept, grad):
    return (grad,)

def back_keep(v):
    return (v, None)

def back_low(kept, grad):
    return (low(grad),)
low.defvjp(low_keep, low_pass)
low_back.defvjp(back_keep, back_low)
epsilon = 1e-06
precise = lax.Precision.HIGHEST

def rms_scale(values):
    return lax.rsqrt(lax.optimization_barrier(jnp.mean(values * values, axis=-1, keepdims=True)) + epsilon)

def row_layer(row_tokens, row_lengths, row_picks, weights):
    w_router, gain_attn, w_qkv, w_out, gain_mlp, w_up, b_up, w_down, b_down = weights
    doc_ends = jnp.cumsum(row_lengths)
    segment = lax.optimization_barrier(jnp.sum((row_picks[:, None] >= doc_ends[None, :]).astype(jnp.int32), axis=1))
    live_mask = (row_picks < doc_ends[-1]).astype(jnp.float32)
    picked = row_tokens[row_picks]
    router = lax.optimization_barrier(jnp.sum(picked * w_router, axis=-1))
    normed = low(picked * rms_scale(picked) * gain_attn)
    qkv_rows = low(low_back(jnp.dot(normed, w_qkv, precision=precise)))
    query_rows = qkv_rows[:, :D].reshape(SEL, HEADS, HEAD)
    key_rows = qkv_rows[:, D:2 * D].reshape(SEL, HEADS, HEAD)
    value_rows = qkv_rows[:, 2 * D:].reshape(SEL, HEADS, HEAD)
    scores = low_back(jnp.einsum('qhe,khe->hqk', query_rows, key_rows, precision=precise) * 0.125)
    position = jnp.arange(SEL)
    allowed = (position[:, None] >= position[None, :]) & (segment[:, None] == segment[None, :])
    scores = jnp.where(allowed[None], scores, -1e+30)
    row_top = lax.optimization_barrier(jnp.max(scores, axis=-1, keepdims=True))
    exponent = jnp.exp(scores - row_top)
    attn_probs = low(exponent / lax.optimization_barrier(jnp.sum(exponent, axis=-1, keepdims=True)))
    attended = jnp.einsum('hqk,khe->qhe', attn_probs, value_rows, precision=precise).reshape(SEL, D)
    attended = low(low_back(attended))
    branch = low_back(jnp.dot(attended, w_out, precision=precise))
    hidden = picked + router[:, None] * branch
    normed_mlp = low(hidden * rms_scale(hidden) * gain_mlp)
    upward = low_back(jnp.dot(normed_mlp, w_up, precision=precise) + b_up)
    active = low(jax.nn.gelu(upward))
    mixed_out = low_back(jnp.dot(active, w_down, precision=precise) + b_down)
    result = hidden + mixed_out
    update = (result - picked) * live_mask[:, None]
    return row_tokens.at[row_picks].add(update)

def reference(tokens, doc_lengths, selected, w_router, gain_attn, w_qkv, w_out, gain_mlp, w_up, b_up, w_down, b_down, cotangent):
    weights = tuple((p.astype(jnp.float32) for p in (w_router, gain_attn, w_qkv, w_out, gain_mlp, w_up, b_up, w_down, b_down)))
    zero_grads = tuple((jnp.zeros(p.shape, jnp.float32) for p in weights))

    def one_row(carry, row):
        sums, live_total = carry
        row_tokens, row_lengths, row_picks, row_cotangent = row

        def forward(tokens_in, weights_in):
            return row_layer(tokens_in, row_lengths, row_picks, weights_in)
        out_row, pullback = jax.vjp(forward, row_tokens.astype(jnp.float32), weights)
        grad_row, grad_weights = pullback(row_cotangent.astype(jnp.float32))
        live_now = jnp.sum((row_picks < jnp.sum(row_lengths)).astype(jnp.float32))
        sums = tuple((a + b for a, b in zip(sums, grad_weights)))
        return ((sums, live_total + live_now), (out_row.astype(jnp.bfloat16), grad_row.astype(jnp.bfloat16)))
    (sums, live_total), (block_out, grad_tokens) = lax.scan(one_row, (zero_grads, jnp.zeros((), jnp.float32)), (tokens, doc_lengths, selected, cotangent))
    means = [s / live_total for s in sums]
    return (block_out, grad_tokens, means[0], means[1], means[2], means[3], means[4], means[5], means[6], means[7], means[8])
```

```python
import functools

import jax
import jax.numpy as jnp
from jax import lax
from jax.experimental import pallas as pl
from jax.experimental.pallas import tpu as pltpu
from jax.sharding import PartitionSpec as P

HEADS = 12
HEAD = 64
EPS = 1e-06
CHUNK = 2048
GROUP = 3 * CHUNK
PIECE = 512
BIG = -1e30
GELU_A = 0.7978845608028654
GELU_B = 0.044715
ROUNDS = {1: 0, 2: 1, 4: 3}
MESH = pl.DeviceIdType.MESH
F32 = jnp.float32
BF16 = jnp.bfloat16


def nn(a, b):
    return lax.dot_general(a, b, (((1,), (0,)), ((), ())), preferred_element_type=F32)


def nt(a, b):
    return lax.dot_general(a, b, (((1,), (1,)), ((), ())), preferred_element_type=F32)


def tn(a, b):
    return lax.dot_general(a, b, (((0,), (0,)), ((), ())), preferred_element_type=F32)


def lanes(shape):
    return lax.broadcasted_iota(jnp.int32, shape, len(shape) - 1)


def row_mean(v):
    return jnp.mean(v, axis=-1, keepdims=True)


def colsum(v):
    total = jnp.sum(v, axis=0, keepdims=True)
    return jnp.concatenate([total[:, j : j + 128] for j in range(0, v.shape[1], 128)], axis=0)


def when(cond, act):
    if cond is None:
        act()
    else:
        pl.when(cond)(act)


def at8(v):
    return v if isinstance(v, int) else pl.multiple_of(v, 8)


def first_kernel(
    lens, sel_col, sel_row, tokens, cot, w_router, gain_attn, w_qkv, w_out, gain_mlp,
    picked_o, cot_o, dmix_o, normed_o, qkv_o, att_o, cols_o, bias_o, branch_o, nm_o, live_o,
):
    r = pl.program_id(0)
    sel, selr = sel_col[0], sel_row[0]
    chosen = sel.shape[0]
    end = jnp.int32(0)
    seg = jnp.zeros(sel.shape, jnp.int32)
    segr = jnp.zeros(selr.shape, jnp.int32)
    for d in range(lens.shape[1]):
        end = end + lens[r, d]
        seg = seg + (sel >= end).astype(jnp.int32)
        segr = segr + (selr >= end).astype(jnp.int32)
    live = (sel < end).astype(F32)
    count = jnp.broadcast_to(jnp.sum(live), live_o.shape)

    @pl.when(r == 0)
    def _():
        live_o[...] = count

    @pl.when(r > 0)
    def _():
        live_o[...] += count

    spots = tokens.shape[1]
    hot = jnp.where(lanes((chosen, spots)) == sel, 1.0, 0.0).astype(BF16)
    picked = nn(hot, tokens[0])
    cot_rows = nn(hot, cot[0])
    picked_o[...] = picked.astype(BF16)
    cot_o[...] = cot_rows.astype(BF16)
    dmix_o[...] = (cot_rows * live).astype(BF16)
    router = jnp.sum(picked * w_router[...].astype(F32), axis=-1, keepdims=True)
    scale_attn = lax.rsqrt(row_mean(picked * picked) + EPS)
    normed = (picked * scale_attn * gain_attn[...].astype(F32)).astype(BF16)
    normed_o[...] = normed
    qkv_o[...] = nn(normed, w_qkv[...]).astype(BF16)
    width = picked.shape[1]
    causal = lanes((chosen, chosen)) <= lax.broadcasted_iota(jnp.int32, (chosen, chosen), 0)
    bias_o[...] = jnp.where(causal & (seg == segr), 0.0, BIG).astype(BF16)
    lane = lanes((chosen, 128))
    is_low = lane < HEAD
    cols = jnp.zeros((chosen, 128), F32)
    for pair in range(HEADS // 2):
        q = qkv_o[:, pair * 128 : pair * 128 + 128]
        k = qkv_o[:, width + pair * 128 : width + pair * 128 + 128]
        v = qkv_o[:, 2 * width + pair * 128 : 2 * width + pair * 128 + 128]
        outs = []
        for a in range(2):
            keep = jnp.where(is_low if a == 0 else ~is_low, HEAD**-0.5, 0.0).astype(BF16)
            scores = nt(q * keep, k) + bias_o[...].astype(F32)
            top = jnp.max(scores, axis=-1, keepdims=True)
            exponent = jnp.exp(scores - top)
            total = jnp.sum(exponent, axis=-1, keepdims=True)
            outs.append(nn((exponent * (1.0 / total)).astype(BF16), v))
            cols = jnp.where(lane == 2 * pair + a, top + jnp.log(total), cols)
        att_o[:, pair * 128 : pair * 128 + 128] = jnp.where(is_low, outs[0], outs[1]).astype(BF16)
    branch = nn(att_o[...], w_out[...])
    branch_o[...] = branch
    hidden = picked + router * branch
    scale_mlp = lax.rsqrt(row_mean(hidden * hidden) + EPS)
    nm_o[...] = (hidden * scale_mlp * gain_mlp[...].astype(F32)).astype(BF16)
    for at, col in enumerate((router, live, scale_attn, scale_mlp)):
        cols = jnp.where(lane == HEADS + at, col, cols)
    cols_o[...] = cols


def first(tokens, doc_lengths, selected, cotangent, w_router, gain_attn, w_qkv, w_out, gain_mlp):
    rows, spots, width = tokens.shape
    chosen = selected.shape[1]
    n = rows * chosen

    def whole(a):
        return pl.BlockSpec(a.shape, lambda r: (0,) * a.ndim)

    def out(cols, kind):
        return jax.ShapeDtypeStruct((n, cols), kind), pl.BlockSpec((chosen, cols), lambda r: (r, 0))

    outs = [
        out(width, BF16), out(width, BF16), out(width, BF16), out(width, BF16), out(3 * width, BF16),
        out(width, BF16), out(128, F32), out(chosen, BF16), out(width, F32), out(width, BF16),
        (jax.ShapeDtypeStruct((8, 128), F32), pl.BlockSpec((8, 128), lambda r: (0, 0))),
    ]
    return pl.pallas_call(
        first_kernel,
        grid=(rows,),
        in_specs=[
            pl.BlockSpec(memory_space=pltpu.SMEM),
            pl.BlockSpec((1, chosen, 1), lambda r: (r, 0, 0)),
            pl.BlockSpec((1, 1, chosen), lambda r: (r, 0, 0)),
            pl.BlockSpec((1, spots, width), lambda r: (r, 0, 0)),
            pl.BlockSpec((1, spots, width), lambda r: (r, 0, 0)),
            whole(w_router), whole(gain_attn), whole(w_qkv), whole(w_out), whole(gain_mlp),
        ],
        out_specs=[o[1] for o in outs],
        out_shape=[o[0] for o in outs],
        compiler_params=pltpu.CompilerParams(vmem_limit_bytes=50 * 2**20),
    )(
        doc_lengths, selected[:, :, None], selected[:, None, :], tokens, cotangent,
        w_router, gain_attn, w_qkv, w_out, gain_mlp,
    )


class Line:
    def __init__(self, n, q, peer):
        self.n, self.q, self.peer = n, q, peer
        self.rounds = ROUNDS[n]
        if n == 4:
            self.side = q // 2
            self.inner = (q == 1) | (q == 2)
            self.outer = jnp.logical_not(self.inner)

    def rs_send(self, r, size):
        h, s = size // self.n, self.q if self.n == 2 else getattr(self, "side", 0)
        if self.n == 2:
            return None, (1 - s) * h, h, self.peer(1 - s)
        if r == 0:
            return self.outer, (1 - s) * h, 3 * h, self.peer(1 + s)
        if r == 1:
            return self.inner, (1 - s) * 2 * h, 2 * h, self.peer(2 - s)
        return self.inner, s * 3 * h, h, self.peer(3 * s)

    def rs_recv(self, r, size):
        h, s = size // self.n, self.q if self.n == 2 else getattr(self, "side", 0)
        if self.n == 2:
            return None, s * h, h
        if r == 0:
            return self.inner, (1 - s) * h, 3 * h
        if r == 1:
            return self.inner, s * 2 * h, 2 * h
        return self.outer, s * 3 * h, h

    def ag_send(self, r, size):
        h, s = size // self.n, self.q if self.n == 2 else getattr(self, "side", 0)
        if self.n == 2:
            return None, s * h, h, self.peer(1 - s)
        if r == 0:
            return self.outer, s * 3 * h, h, self.peer(1 + s)
        if r == 1:
            return self.inner, s * 2 * h, 2 * h, self.peer(2 - s)
        return self.inner, (1 - s) * h, 3 * h, self.peer(3 * s)

    def ag_recv(self, r, size):
        h, s = size // self.n, self.q if self.n == 2 else getattr(self, "side", 0)
        if self.n == 2:
            return None, (1 - s) * h, h
        if r == 0:
            return self.inner, s * 3 * h, h
        if r == 1:
            return self.inner, (1 - s) * 2 * h, 2 * h
        return self.outer, (1 - s) * h, 3 * h


def recv_rows(sizes, rows):
    total = 0
    for n in sizes:
        rows = rows // n
        total += {1: 0, 2: 1, 4: 5}[n] * rows
    return total


class Part:
    def __init__(self, lines, rows):
        self.steps = []
        base, size, slot = 0, rows, 0
        levels = []
        for ln in lines:
            h = size // ln.n
            offs = {1: [], 2: [slot], 4: [slot, slot + 3 * h, slot]}[ln.n]
            slot += {1: 0, 2: 1, 4: 5}[ln.n] * h
            levels.append((ln, base, size))
            for r in range(ln.rounds):
                self.steps.append(("rs", ln, r, base, size, offs[r]))
            if ln.n > 1:
                base = base + ln.q * h
            size = h
        self.own = (base, size)
        self.n_rs = len(self.steps)
        for ln, b, s in reversed(levels):
            for r in range(ln.rounds):
                self.steps.append(("ag", ln, r, b, s, None))


def lags_of(n_steps):
    lags = [0]
    for k in range(n_steps):
        lags.append(lags[-1] + (2 if k < 2 or k >= n_steps - 2 else 1))
    return lags


def sums_kernel(
    cfg,
    nm_h, dmix_h, normed_h, qkv_h, att_h, cols_h, bias_h, branch_h, picked_h, cot_h, w_up_h, w_down_h, w_qkv_h, w_out_h,
    live_in, b_up, b_down, w_router, gain_attn, gain_mlp,
    sums, small_o, new_block, new_grad,
    nm, nm_t, dmix, w_up, w_down, act, slope, d_up, mixed, d_nm, qkv, att, cols, bias, branch, picked, cot, w_qkv, w_out,
    stage, cbuf, acc, rbuf, vecs, live_s, tiny,
    load_sem, w_sem, row_sem, out_sem, c_send, c_recv, x_send, x_recv, own_sem, f_send, f_recv, t_send, t_recv,
):
    n0, n1, n2 = cfg["dims"]
    lags, n_chunks, n_small = cfg["lags"], cfg["chunks"], cfg["small"]
    n_steps, slots = len(lags) - 1, acc.shape[0]
    dp, sub = lax.axis_index("dp"), lax.axis_index("sub")
    q2, q1, q0 = dp % n2, (dp // n2) % n1, dp // (n2 * n1)

    def chip(a, b, c):
        return (a * (n1 * n2) + b * n2 + c, sub)

    peers = [lambda v: chip(v, q1, q2), lambda v: chip(q0, v, q2), lambda v: chip(q0, q1, v)]
    places = list(zip((n0, n1, n2), (q0, q1, q2), peers, strict=True))
    l0, l1, l2 = (Line(n, q, peer) for n, q, peer in places)
    core = (dp, 1 - sub)
    part_rows = CHUNK // 4
    parts = [Part([l2, l0, l1], part_rows), Part([l1, l0, l2], part_rows)]
    n_rs = parts[0].n_rs
    tokens, width = nm.shape
    chosen = bias.shape[1]
    rows = tokens // chosen
    pieces = w_up_h.shape[1] // PIECE

    loads = [
        pltpu.make_async_copy(src, dst, load_sem.at[i])
        for i, (src, dst) in enumerate(
            (
                (nm_h, nm), (dmix_h, dmix), (qkv_h, qkv), (att_h, att), (cols_h, cols), (bias_h, bias),
                (picked_h, picked), (cot_h, cot), (w_qkv_h, w_qkv), (w_out_h, w_out),
            )
        )
    ]

    def weights_in(f):
        cut = pl.ds(pl.multiple_of(f * PIECE, PIECE), PIECE)
        slot = f % 2
        return (
            pltpu.make_async_copy(w_up_h.at[:, cut], w_up.at[slot], w_sem.at[slot, 0]),
            pltpu.make_async_copy(w_down_h.at[cut], w_down.at[slot], w_sem.at[slot, 1]),
        )

    def branch_in(r):
        return pltpu.make_async_copy(branch_h.at[pl.ds(r * chosen, chosen)], branch.at[r % 2], row_sem.at[r % 2])

    def normed_in():
        return pltpu.make_async_copy(normed_h, nm, load_sem.at[len(loads)])

    for i in range(2):
        loads[i].start()
    for copy in weights_in(0):
        copy.start()

    greeted = [core] + [peer((q + d) % n) for n, q, peer in places for d in range(1, n)]
    barrier = pltpu.get_barrier_semaphore()
    for device in greeted:
        pl.semaphore_signal(barrier, inc=1, device_id=device, device_id_type=MESH)
    mixed[...] = jnp.zeros_like(mixed)
    d_nm[...] = jnp.zeros_like(d_nm)
    for i in range(2):
        loads[i].wait()
    for i in range(2, len(loads)):
        loads[i].start()
    vecs[...] = jnp.zeros_like(vecs)
    for r in range(rows):
        cut = pl.ds(r * chosen, chosen)
        nm_t[:, cut] = nm[cut].T
        vecs[24:30] += colsum(dmix[cut].astype(F32))
    pl.semaphore_wait(barrier, len(greeted))


    def half_out(c):
        j = c % 3
        return pltpu.make_async_remote_copy(
            src_ref=stage.at[pl.ds(at8(j * CHUNK + (1 - sub) * (CHUNK // 2)), CHUNK // 2)], dst_ref=cbuf.at[j],
            send_sem=c_send.at[c], recv_sem=c_recv.at[c], device_id=core, device_id_type=MESH,
        )

    def out_copy(c, p, k):
        kind, ln, r, base, size, slot = parts[p].steps[k]
        who, off, n, device = (ln.rs_send if kind == "rs" else ln.ag_send)(r, size)
        here = pl.ds(at8(p * part_rows + base + off), n)
        if kind == "rs":
            src, dst = acc.at[c % slots, here], rbuf.at[c % slots, p, pl.ds(slot, n)]
        else:
            dst = sums.at[c, sub, here]
            src = acc.at[c % slots, here] if k == n_rs else dst
        return who, pltpu.make_async_remote_copy(
            src_ref=src, dst_ref=dst, send_sem=x_send.at[c, p, k], recv_sem=x_recv.at[c, p, k],
            device_id=device, device_id_type=MESH,
        )

    def own_copy(c, p):
        base, n = parts[p].own
        here = pl.ds(at8(p * part_rows + base), n)
        return pltpu.make_async_copy(acc.at[c % slots, here], sums.at[c, sub, here], own_sem.at[c, p])

    def begin(c, p, k):
        who, copy = out_copy(c, p, k)
        when(who, copy.start)
        if k == n_rs:
            own_copy(c, p).start()

    def finish(c, p, k):
        kind, ln, r, base, size, slot = parts[p].steps[k]
        who, off, n = (ln.rs_recv if kind == "rs" else ln.ag_recv)(r, size)
        here = pl.ds(at8(p * part_rows + base + off), n)
        came = rbuf.at[c % slots, p, pl.ds(slot, n)] if kind == "rs" else sums.at[c, sub, here]

        def take():
            pltpu.make_async_remote_copy(
                src_ref=came, dst_ref=came, send_sem=x_send.at[c, p, k], recv_sem=x_recv.at[c, p, k],
                device_id=core, device_id_type=MESH,
            ).wait_recv()
            if kind == "rs":
                region = acc.at[c % slots, here]
                region[...] = region[...] + came[...]

        when(who, take)
        who, copy = out_copy(c, p, k)
        when(who, copy.wait_send)
        if k == n_rs:
            own_copy(c, p).wait()
        if k == n_rs - 1:
            base, n = parts[p].own
            mine = acc.at[c % slots, pl.ds(at8(p * part_rows + base), n)]
            mine[...] = mine[...] / live_s[0:1]

    def half_back(c, half):
        return pltpu.make_async_remote_copy(
            src_ref=sums.at[c, half], dst_ref=sums.at[c, half], send_sem=f_send.at[c], recv_sem=f_recv.at[c],
            device_id=core, device_id_type=MESH,
        )

    def events(t):
        for k in range(n_steps, -1, -1):
            c = t - 1 - lags[k]

            def event(k=k, c=c):
                for p in range(2):
                    if k > 0:
                        finish(c, p, k - 1)
                    elif p == 0:
                        half_out(c).wait()
                        mine = pl.ds(at8((c % 3) * CHUNK + sub * (CHUNK // 2)), CHUNK // 2)
                        acc[c % slots] = stage[mine] + cbuf[c % 3]
                    if k < n_steps:
                        begin(c, p, k)
                if k == n_steps:
                    half_back(c, sub).start()

            pl.when((c >= 0) & (c < n_chunks))(event)


    pairs = [core]
    for n, q, peer in places:
        bit = 1
        while bit < n:
            pairs.append(peer(q + bit - 2 * bit * ((q // bit) % 2)))
            bit *= 2

    def tiny_copy(which, i):
        here = pl.ds(0, 8) if which == 0 else pl.ds(8, n_small)
        return pltpu.make_async_remote_copy(
            src_ref=tiny.at[0, i, here], dst_ref=tiny.at[1, i, here],
            send_sem=t_send.at[which, i], recv_sem=t_recv.at[which, i], device_id=pairs[i], device_id_type=MESH,
        )

    def tiny_steps(t, first, which, total):
        here = pl.ds(0, 8) if which == 0 else pl.ds(8, n_small)
        for i in range(len(pairs) + 1):

            def step(i=i):
                if i > 0:
                    tiny_copy(which, i - 1).wait()
                    total[...] = total[...] + tiny[1, i - 1, here]
                if i < len(pairs):
                    tiny[0, i, here] = total[...]
                    tiny_copy(which, i).start()
                elif which == 1:
                    small_o[...] = total[...] / live_s[0:1]

            pl.when(t == first + i)(step)


    def put(base, block, value):
        for j in range(value.shape[1] // 128):
            stage[base + j * block : base + (j + 1) * block] = value[:, j * 128 : (j + 1) * 128]

    def piece_up(f):
        for copy in weights_in(f):
            copy.wait()

        def more():
            for copy in weights_in(f + 1):
                copy.start()

        pl.when(f + 1 < pieces)(more)
        slot = f % 2
        b = b_up[:, pl.ds(pl.multiple_of(f * PIECE, PIECE), PIECE)].astype(F32)
        for r in range(rows):
            cut = pl.ds(r * chosen, chosen)
            u = nn(nm[cut], w_up[slot]) + b
            u2 = u * u
            t = jnp.tanh(GELU_A * u * (1.0 + GELU_B * u2))
            act[cut] = (0.5 * u * (1.0 + t)).astype(BF16)
            slope[cut] = 0.5 * (1.0 + t) + 0.5 * u * (1.0 - t * t) * (GELU_A * (1.0 + 3.0 * GELU_B * u2))
        put(0, PIECE, tn(act[...], dmix[...]))

    def piece_back(f):
        slot = f % 2
        sums_b = jnp.zeros((PIECE // 128, 128), F32)
        for r in range(rows):
            cut = pl.ds(r * chosen, chosen)
            d = (nt(dmix[cut], w_down[slot]) * slope[cut]).astype(BF16)
            d_up[cut] = d
            sums_b = sums_b + colsum(d.astype(F32))
        vecs[pl.ds(at8(32 + 8 * f), PIECE // 128)] = sums_b
        put(PIECE * 6, width, nn(nm_t[...], d_up[...]))

    def piece_on(f):
        slot = f % 2
        for r in range(rows):
            cut = pl.ds(r * chosen, chosen)
            mixed[cut] += nn(act[cut], w_down[slot])
            d_nm[cut] += nt(d_up[cut], w_up[slot])


    lane = lanes((chosen, 128))
    is_low = lane < HEAD

    def col(r, at):
        return cols[pl.ds(r * chosen, chosen), at : at + 1]

    def hidden_back():
        for i in range(2, len(loads)):
            loads[i].wait()
        branch_in(0).start()
        for r in range(rows):
            branch_in(r).wait()
            if r + 1 < rows:
                branch_in(r + 1).start()
            cut = pl.ds(r * chosen, chosen)
            br = branch[r % 2]
            x = picked[cut].astype(F32)
            router, live, scale = col(r, HEADS), col(r, HEADS + 1), col(r, HEADS + 3)
            hidden = x + router * br
            unit = hidden * scale
            d_res = dmix[cut].astype(F32)
            dn = d_nm[cut]
            vecs[16:22] += colsum(dn * unit)
            d_unit = dn * gain_mlp[...].astype(F32)
            d_hidden = d_res + scale * (d_unit - unit * row_mean(d_unit * unit))
            dmix[cut] = (x + (hidden + mixed[cut] + b_down[...].astype(F32) - x) * live).astype(BF16)
            d_router = jnp.sum(d_hidden * br, axis=-1, keepdims=True)
            vecs[0:6] += colsum(d_router * x)
            d_branch = (router * d_hidden).astype(BF16)
            nm[cut] = d_branch
            mixed[cut] = d_hidden - d_res + d_router * w_router[...].astype(F32)
        pltpu.make_async_copy(dmix, new_block, out_sem.at[0]).start()
        put(0, width, tn(att[...], nm[...]))
        for r in range(rows):
            cut = pl.ds(r * chosen, chosen)
            att[cut] = nt(nm[cut], w_out[...]).astype(BF16)
        normed_in().start()

    def attention_back(r):
        def one_pair(pair, carry):
            cut = pl.ds(r * chosen, chosen)
            sq = pl.ds(pl.multiple_of(pair * 128, 128), 128)
            sk = pl.ds(pl.multiple_of(width + pair * 128, 128), 128)
            sv = pl.ds(pl.multiple_of(2 * width + pair * 128, 128), 128)
            q, k, v, do = qkv[cut, sq], qkv[cut, sk], qkv[cut, sv], att[cut, sq]
            made = []
            for a in range(2):
                side = is_low if a == 0 else ~is_low
                keep = jnp.where(side, 1.0, 0.0).astype(BF16)
                log_total = jnp.sum(jnp.where(lane == 2 * pair + a, cols[cut], 0.0), axis=-1, keepdims=True)
                probs = jnp.exp(nt(q * keep, k) * HEAD**-0.5 + bias[cut].astype(F32) - log_total)
                d_probs = nt(do * keep, v)
                d_scores = probs * (d_probs - jnp.sum(d_probs * probs, axis=-1, keepdims=True))
                d_scores = d_scores.astype(BF16)
                made.append((nn(d_scores, k), tn(d_scores, q), tn(probs.astype(BF16), do)))
            dq, dk, dv = (jnp.where(is_low, x, y) for x, y in zip(*made, strict=True))
            qkv[cut, sq] = (dq * HEAD**-0.5).astype(BF16)
            qkv[cut, sk] = (dk * HEAD**-0.5).astype(BF16)
            qkv[cut, sv] = dv.astype(BF16)
            return carry

        lax.fori_loop(0, HEADS // 2, one_pair, 0)

    def tokens_back(r):
        cut = pl.ds(r * chosen, chosen)
        d_normed = nt(qkv[cut], w_qkv[...])
        x = picked[cut].astype(F32)
        scale = col(r, HEADS + 2)
        unit = x * scale
        vecs[8:14] += colsum(d_normed * unit)
        d_unit = d_normed * gain_attn[...].astype(F32)
        d_picked = mixed[cut] + scale * (d_unit - unit * row_mean(d_unit * unit))
        cot[cut] = (cot[cut].astype(F32) + d_picked).astype(BF16)

    def compute(t):
        @pl.when(t < 3 * pieces)
        def _():
            f = t // 3
            pl.when(t % 3 == 0)(lambda: piece_up(f))
            pl.when(t % 3 == 1)(lambda: piece_back(f))
            pl.when(t % 3 == 2)(lambda: piece_on(f))

        t0 = 3 * pieces
        pl.when(t == t0)(hidden_back)

        @pl.when(t == t0 + 1)
        def _():
            for r in range(rows // 2):
                attention_back(r)

        @pl.when(t == t0 + 2)
        def _():
            for r in range(rows // 2, rows):
                attention_back(r)
            normed_in().wait()
            put(6 * width, width, tn(nm[...], qkv[:, 0:256]))

        @pl.when(t == t0 + 3)
        def _():
            put(0, width, tn(nm[...], qkv[:, 256:1280]))

        @pl.when(t == t0 + 6)
        def _():
            put(0, width, tn(nm[...], qkv[:, 1280:2304]))

        @pl.when(t == t0 + 8)
        def _():
            for r in range(rows):
                tokens_back(r)
            pltpu.make_async_copy(cot, new_grad, out_sem.at[1]).start()

    live_s[...] = live_in[...]

    def tick(t, carry):
        events(t)
        compute(t)
        pl.when(t < n_chunks)(lambda: half_out(t).start())
        tiny_steps(t, 0, 0, live_s)
        tiny_steps(t, n_chunks, 1, vecs)
        return carry

    lax.fori_loop(0, n_chunks + lags[-1] + 1, tick, 0)

    def last(c, carry):
        half_back(c, sub).wait_send()
        half_back(c, 1 - sub).wait_recv()
        return carry

    lax.fori_loop(0, n_chunks, last, 0)
    pltpu.make_async_copy(dmix, new_block, out_sem.at[0]).wait()
    pltpu.make_async_copy(cot, new_grad, out_sem.at[1]).wait()


def device_sums(mesh, made, weights, vectors):
    picked, cot, dmix, normed, qkv, att, cols, bias, branch, nm, live = made
    w_qkv, w_out, w_up, w_down = weights
    tokens, width = nm.shape
    chosen = bias.shape[1]
    hidden = w_up.shape[1]
    dims = {16: (4, 2, 2), 64: (4, 4, 4)}[mesh.shape["dp"]]
    n_steps = 2 * sum(ROUNDS[n] for n in dims)
    lags = lags_of(n_steps)
    slots = lags[n_steps // 2 + 1] + 1
    chunks = (2 * width * hidden + width * width * 4) // (128 * CHUNK)
    part_rows = CHUNK // 4
    came = max(recv_rows(order, part_rows) for order in ((dims[2], dims[0], dims[1]), (dims[1], dims[0], dims[2])))
    n_tiny = 1 + sum({1: 0, 2: 1, 4: 2}[n] for n in dims)
    n_small = 32 + 8 * (hidden // PIECE)
    vmem, dma = pltpu.VMEM, pltpu.SemaphoreType.DMA
    big = pl.BlockSpec(memory_space=pl.ANY)
    near = pl.BlockSpec(memory_space=vmem)
    return pl.pallas_call(
        functools.partial(sums_kernel, dict(dims=dims, lags=lags, chunks=chunks, small=n_small)),
        in_specs=[big] * 14 + [near] * 6,
        out_specs=[big, near, big, big],
        out_shape=[
            jax.ShapeDtypeStruct((chunks, 2, CHUNK // 2, 128), F32),
            jax.ShapeDtypeStruct((n_small, 128), F32),
            jax.ShapeDtypeStruct((tokens, width), BF16),
            jax.ShapeDtypeStruct((tokens, width), BF16),
        ],
        scratch_shapes=[
            vmem((tokens, width), BF16),
            vmem((width, tokens), BF16),
            vmem((tokens, width), BF16),
            vmem((2, width, PIECE), BF16),
            vmem((2, PIECE, width), BF16),
            vmem((tokens, PIECE), BF16),
            vmem((tokens, PIECE), F32),
            vmem((tokens, PIECE), BF16),
            vmem((tokens, width), F32),
            vmem((tokens, width), F32),
            vmem((tokens, 3 * width), BF16),
            vmem((tokens, width), BF16),
            vmem((tokens, 128), F32),
            vmem((tokens, chosen), BF16),
            vmem((2, chosen, width), F32),
            vmem((tokens, width), BF16),
            vmem((tokens, width), BF16),
            vmem((width, 3 * width), BF16),
            vmem((width, width), BF16),
            vmem((3 * CHUNK, 128), F32),
            vmem((3, CHUNK // 2, 128), F32),
            vmem((slots, CHUNK // 2, 128), F32),
            vmem((slots, 2, came, 128), F32),
            vmem((n_small, 128), F32),
            vmem((8, 128), F32),
            vmem((2, n_tiny, n_small + 8, 128), F32),
            dma((11,)),
            dma((2, 2)),
            dma((2,)),
            dma((2,)),
            dma((chunks,)),
            dma((chunks,)),
            dma((chunks, 2, n_steps)),
            dma((chunks, 2, n_steps)),
            dma((chunks, 2)),
            dma((chunks,)),
            dma((chunks,)),
            dma((2, n_tiny)),
            dma((2, n_tiny)),
        ],
        compiler_params=pltpu.CompilerParams(collective_id=0, has_side_effects=True, vmem_limit_bytes=60 * 2**20),
    )(nm, dmix, normed, qkv, att, cols, bias, branch, picked, cot, w_up, w_down, w_qkv, w_out, live, *vectors)


def last_kernel(
    sel_row, tokens, cot, new_block, new_grad, sums,
    block_out, grad_tokens, grad_qkv, grad_out, grad_up, grad_down, near, in_sems, sems,
):
    step = pl.program_id(0) * pl.num_programs(1) + pl.program_id(1)
    width, hidden = grad_up.shape
    copies = []

    def copy(row, n, dst):
        copies.append((row // GROUP, pltpu.make_async_copy(near.at[pl.ds(row, n)], dst, sems.at[len(copies)])))
        return row + n

    row = 0
    for f in range(0, hidden, PIECE):
        for j in range(0, width, 128):
            row = copy(row, PIECE, grad_down.at[pl.ds(f, PIECE), pl.ds(j, 128)])
        for j in range(f, f + PIECE, 128):
            row = copy(row, width, grad_up.at[:, pl.ds(j, 128)])
    for j in range(0, width, 128):
        row = copy(row, width, grad_out.at[:, pl.ds(j, 128)])
    for j in range(0, 3 * width, 128):
        row = copy(row, width, grad_qkv.at[:, pl.ds(j, 128)])

    groups = sums.shape[0] // GROUP
    fetch = [
        pltpu.make_async_copy(sums.at[pl.ds(g * GROUP, GROUP)], near.at[pl.ds(g * GROUP, GROUP)], in_sems.at[g])
        for g in range(groups)
    ]
    steps = pl.num_programs(0) * pl.num_programs(1)

    @pl.when(step == 0)
    def _():
        for f in fetch:
            f.start()

    for g in range(groups):

        @pl.when(step == jnp.minimum(g, steps - 1))
        def _(g=g):
            fetch[g].wait()
            for at, c in copies:
                if at == g:
                    c.start()

    spots = tokens.shape[1]
    sel = sel_row[0]
    spot = lax.broadcasted_iota(jnp.int32, (spots, sel.shape[1]), 0) + pl.program_id(1) * spots
    hot = jnp.where(spot == sel, 1.0, 0.0)
    hit = jnp.max(hot, axis=-1, keepdims=True) > 0.0
    hot = hot.astype(BF16)
    for old, new, out in ((tokens, new_block, block_out), (cot, new_grad, grad_tokens)):
        fresh = nn(hot, new[...])
        out[0] = jnp.where(hit, fresh, old[0].astype(F32)).astype(BF16)

    @pl.when(step == steps - 1)
    def _():
        for _, c in copies:
            c.wait()


def last(tokens, cotangent, selected, new_block, new_grad, sums, hidden):
    rows, spots, width = tokens.shape
    chosen = selected.shape[1]
    cut = 1024
    big = pl.BlockSpec(memory_space=pl.ANY)
    table = pl.BlockSpec((1, cut, width), lambda r, i: (r, i, 0))
    fresh = pl.BlockSpec((chosen, width), lambda r, i: (r, 0))
    n_copies = hidden // PIECE * (width // 128) + hidden // 128 + 4 * (width // 128)
    return pl.pallas_call(
        last_kernel,
        grid=(rows, spots // cut),
        in_specs=[pl.BlockSpec((1, 1, chosen), lambda r, i: (r, 0, 0)), table, table, fresh, fresh, big],
        out_specs=[table, table, big, big, big, big],
        out_shape=[
            jax.ShapeDtypeStruct(tokens.shape, BF16),
            jax.ShapeDtypeStruct(tokens.shape, BF16),
            jax.ShapeDtypeStruct((width, 3 * width), F32),
            jax.ShapeDtypeStruct((width, width), F32),
            jax.ShapeDtypeStruct((width, hidden), F32),
            jax.ShapeDtypeStruct((hidden, width), F32),
        ],
        scratch_shapes=[
            pltpu.VMEM(sums.shape, F32),
            pltpu.SemaphoreType.DMA((sums.shape[0] // GROUP,)),
            pltpu.SemaphoreType.DMA((n_copies,)),
        ],
        compiler_params=pltpu.CompilerParams(vmem_limit_bytes=50 * 2**20),
    )(selected[:, None, :], tokens, cotangent, new_block, new_grad, sums)


def body(
    mesh, tokens, doc_lengths, selected, w_router, gain_attn, w_qkv, w_out, gain_mlp, w_up, b_up, w_down, b_down, cotangent
):
    hidden = w_up.shape[1]
    w_router, gain_attn, gain_mlp, b_up, b_down = (v[None] for v in (w_router, gain_attn, gain_mlp, b_up, b_down))
    made = first(tokens, doc_lengths, selected, cotangent, w_router, gain_attn, w_qkv, w_out, gain_mlp)
    sums, small, new_block, new_grad = device_sums(
        mesh, made, (w_qkv, w_out, w_up, w_down), (b_up, b_down, w_router, gain_attn, gain_mlp)
    )
    block_out, grad_tokens, grad_qkv, grad_out, grad_up, grad_down = last(
        tokens, cotangent, selected, new_block, new_grad, sums.reshape(-1, 128), hidden
    )
    grad_b_up = small[32:].reshape(-1, 8, 128)[:, : PIECE // 128].reshape(-1)
    grad_router, grad_gain_attn, grad_gain_mlp, grad_b_down = (small[i : i + 6].reshape(-1) for i in (0, 8, 16, 24))
    return (
        block_out,
        grad_tokens,
        grad_router,
        grad_gain_attn,
        grad_qkv,
        grad_out,
        grad_gain_mlp,
        grad_up,
        grad_b_up,
        grad_down,
        grad_b_down,
    )


def solution(mesh):
    split, copied = P(("dp", "sub")), P()
    return jax.shard_map(
        functools.partial(body, mesh),
        mesh=mesh,
        in_specs=(split,) * 3 + (copied,) * 9 + (split,),
        out_specs=(split,) * 2 + (copied,) * 9,
        check_vma=False,
    )
```

```python
import functools

import jax
import jax.numpy as jnp
from jax import lax
from jax.experimental import pallas as pl
from jax.experimental.pallas import tpu as pltpu
from jax.sharding import PartitionSpec as P

HEADS = 12
HEAD = 64
EPS = 1e-06
CHUNK = 2048
GROUP = 3 * CHUNK
PIECE = 512
BIG = -1e30
GELU_A = 0.7978845608028654
GELU_B = 0.044715
ROUNDS = {1: 0, 2: 1, 4: 3}
MESH = pl.DeviceIdType.MESH
F32 = jnp.float32
BF16 = jnp.bfloat16


def nn(a, b):
    return lax.dot_general(a, b, (((1,), (0,)), ((), ())), preferred_element_type=F32)


def nt(a, b):
    return lax.dot_general(a, b, (((1,), (1,)), ((), ())), preferred_element_type=F32)


def tn(a, b):
    return lax.dot_general(a, b, (((0,), (0,)), ((), ())), preferred_element_type=F32)


def vector(ref):
    return ref[...].astype(F32)[None]


def lanes(shape):
    return lax.broadcasted_iota(jnp.int32, shape, len(shape) - 1)


def row_mean(v):
    return jnp.mean(v, axis=-1, keepdims=True)


def colsum(v):
    total = jnp.sum(v, axis=0, keepdims=True)
    return jnp.concatenate([total[:, j : j + 128] for j in range(0, v.shape[1], 128)], axis=0)


def when(cond, act):
    if cond is None:
        act()
    else:
        pl.when(cond)(act)


def at8(v):
    return v if isinstance(v, int) else pl.multiple_of(v, 8)


def first_kernel(
    lens, selected, tokens, cot, w_router, gain_attn, w_qkv, w_out, gain_mlp,
    picked_o, cot_o, dmix_o, normed_o, qkv_o, att_o, cols_o, bias_o, branch_o, nm_o, live_o,
):
    r = pl.program_id(0)
    chosen = selected.shape[1]
    selr = selected[pl.ds(r, 1)]
    diagonal = lanes((chosen, chosen)) == lax.broadcasted_iota(jnp.int32, (chosen, chosen), 0)
    sel = jnp.sum(jnp.where(diagonal, selr.astype(F32), 0.0), axis=-1, keepdims=True).astype(jnp.int32)
    end = jnp.int32(0)
    seg = jnp.zeros(sel.shape, jnp.int32)
    segr = jnp.zeros(selr.shape, jnp.int32)
    for d in range(lens.shape[1]):
        end = end + lens[r, d]
        seg = seg + (sel >= end).astype(jnp.int32)
        segr = segr + (selr >= end).astype(jnp.int32)
    live = (sel < end).astype(F32)
    count = jnp.broadcast_to(jnp.sum(live), live_o.shape)

    @pl.when(r == 0)
    def _():
        live_o[...] = count

    @pl.when(r > 0)
    def _():
        live_o[...] += count

    spots = tokens.shape[1]
    hot = jnp.where(lanes((chosen, spots)) == sel, 1.0, 0.0).astype(BF16)
    picked = nn(hot, tokens[0])
    cot_rows = nn(hot, cot[0])
    picked_o[...] = picked.astype(BF16)
    cot_o[...] = cot_rows.astype(BF16)
    dmix_o[...] = (cot_rows * live).astype(BF16)
    router = jnp.sum(picked * vector(w_router), axis=-1, keepdims=True)
    scale_attn = lax.rsqrt(row_mean(picked * picked) + EPS)
    normed = (picked * scale_attn * vector(gain_attn)).astype(BF16)
    normed_o[...] = normed
    qkv_o[...] = nn(normed, w_qkv[...]).astype(BF16)
    width = picked.shape[1]
    causal = lanes((chosen, chosen)) <= lax.broadcasted_iota(jnp.int32, (chosen, chosen), 0)
    bias_o[...] = jnp.where(causal & (seg == segr), 0.0, BIG).astype(BF16)
    lane = lanes((chosen, 128))
    is_low = lane < HEAD
    cols = jnp.zeros((chosen, 128), F32)
    for pair in range(HEADS // 2):
        q = qkv_o[:, pair * 128 : pair * 128 + 128]
        k = qkv_o[:, width + pair * 128 : width + pair * 128 + 128]
        v = qkv_o[:, 2 * width + pair * 128 : 2 * width + pair * 128 + 128]
        outs = []
        for a in range(2):
            keep = jnp.where(is_low if a == 0 else ~is_low, HEAD**-0.5, 0.0).astype(BF16)
            scores = nt(q * keep, k) + bias_o[...].astype(F32)
            top = jnp.max(scores, axis=-1, keepdims=True)
            exponent = jnp.exp(scores - top)
            total = jnp.sum(exponent, axis=-1, keepdims=True)
            outs.append(nn((exponent * (1.0 / total)).astype(BF16), v))
            cols = jnp.where(lane == 2 * pair + a, top + jnp.log(total), cols)
        att_o[:, pair * 128 : pair * 128 + 128] = jnp.where(is_low, outs[0], outs[1]).astype(BF16)
    branch = nn(att_o[...], w_out[...])
    branch_o[...] = branch
    hidden = picked + router * branch
    scale_mlp = lax.rsqrt(row_mean(hidden * hidden) + EPS)
    nm_o[...] = (hidden * scale_mlp * vector(gain_mlp)).astype(BF16)
    for at, col in enumerate((router, live, scale_attn, scale_mlp)):
        cols = jnp.where(lane == HEADS + at, col, cols)
    cols_o[...] = cols


def first(tokens, doc_lengths, selected, cotangent, w_router, gain_attn, w_qkv, w_out, gain_mlp):
    rows, spots, width = tokens.shape
    chosen = selected.shape[1]
    n = rows * chosen

    def whole(a):
        return pl.BlockSpec(a.shape, lambda r: (0,) * a.ndim)

    def out(cols, kind):
        return jax.ShapeDtypeStruct((n, cols), kind), pl.BlockSpec((chosen, cols), lambda r: (r, 0))

    outs = [
        out(width, BF16), out(width, BF16), out(width, BF16), out(width, BF16), out(3 * width, BF16),
        out(width, BF16), out(128, F32), out(chosen, BF16), out(width, F32), out(width, BF16),
        (jax.ShapeDtypeStruct((8, 128), F32), pl.BlockSpec((8, 128), lambda r: (0, 0))),
    ]
    return pl.pallas_call(
        first_kernel,
        grid=(rows,),
        in_specs=[
            pl.BlockSpec(memory_space=pltpu.SMEM),
            whole(selected),
            pl.BlockSpec((1, spots, width), lambda r: (r, 0, 0)),
            pl.BlockSpec((1, spots, width), lambda r: (r, 0, 0)),
            whole(w_router), whole(gain_attn), whole(w_qkv), whole(w_out), whole(gain_mlp),
        ],
        out_specs=[o[1] for o in outs],
        out_shape=[o[0] for o in outs],
        compiler_params=pltpu.CompilerParams(vmem_limit_bytes=63 * 2**20),
    )(
        doc_lengths, selected, tokens, cotangent,
        w_router, gain_attn, w_qkv, w_out, gain_mlp,
    )


class Line:
    def __init__(self, n, q, peer):
        self.n, self.q, self.peer = n, q, peer
        self.rounds = ROUNDS[n]
        if n == 4:
            self.side = q // 2
            self.inner = (q == 1) | (q == 2)
            self.outer = jnp.logical_not(self.inner)

    def rs_send(self, r, size):
        h, s = size // self.n, self.q if self.n == 2 else getattr(self, "side", 0)
        if self.n == 2:
            return None, (1 - s) * h, h, self.peer(1 - s)
        if r == 0:
            return self.outer, (1 - s) * h, 3 * h, self.peer(1 + s)
        if r == 1:
            return self.inner, (1 - s) * 2 * h, 2 * h, self.peer(2 - s)
        return self.inner, s * 3 * h, h, self.peer(3 * s)

    def rs_recv(self, r, size):
        h, s = size // self.n, self.q if self.n == 2 else getattr(self, "side", 0)
        if self.n == 2:
            return None, s * h, h
        if r == 0:
            return self.inner, (1 - s) * h, 3 * h
        if r == 1:
            return self.inner, s * 2 * h, 2 * h
        return self.outer, s * 3 * h, h

    def ag_send(self, r, size):
        h, s = size // self.n, self.q if self.n == 2 else getattr(self, "side", 0)
        if self.n == 2:
            return None, s * h, h, self.peer(1 - s)
        if r == 0:
            return self.outer, s * 3 * h, h, self.peer(1 + s)
        if r == 1:
            return self.inner, s * 2 * h, 2 * h, self.peer(2 - s)
        return self.inner, (1 - s) * h, 3 * h, self.peer(3 * s)

    def ag_recv(self, r, size):
        h, s = size // self.n, self.q if self.n == 2 else getattr(self, "side", 0)
        if self.n == 2:
            return None, (1 - s) * h, h
        if r == 0:
            return self.inner, s * 3 * h, h
        if r == 1:
            return self.inner, (1 - s) * 2 * h, 2 * h
        return self.outer, (1 - s) * h, 3 * h


def recv_rows(sizes, rows):
    total = 0
    for n in sizes:
        rows = rows // n
        total += {1: 0, 2: 1, 4: 5}[n] * rows
    return total


class Part:
    def __init__(self, lines, rows):
        self.steps = []
        base, size, slot = 0, rows, 0
        levels = []
        for ln in lines:
            h = size // ln.n
            offs = {1: [], 2: [slot], 4: [slot, slot + 3 * h, slot]}[ln.n]
            slot += {1: 0, 2: 1, 4: 5}[ln.n] * h
            levels.append((ln, base, size))
            for r in range(ln.rounds):
                self.steps.append(("rs", ln, r, base, size, offs[r]))
            if ln.n > 1:
                base = base + ln.q * h
            size = h
        self.own = (base, size)
        self.n_rs = len(self.steps)
        for ln, b, s in reversed(levels):
            for r in range(ln.rounds):
                self.steps.append(("ag", ln, r, b, s, None))


def lags_of(n_steps):
    lags = [0]
    for k in range(n_steps):
        lags.append(lags[-1] + (2 if k < 2 or k >= n_steps - 2 else 1))
    return lags


def sums_kernel(
    cfg,
    nm_h, dmix_h, normed_h, qkv_h, att_h, cols_h, bias_h, branch_h, picked_h, cot_h, w_up_h, w_down_h, w_qkv_h, w_out_h,
    live_in, b_up, b_down, w_router, gain_attn, gain_mlp,
    sums, small_o, new_block, new_grad,
    nm, nm_t, dmix, w_up, w_down, act, slope, d_up, mixed, d_nm, qkv, att, cols, bias, branch, picked, cot, w_qkv, w_out,
    stage, cbuf, acc, rbuf, vecs, live_s, tiny,
    load_sem, w_sem, row_sem, out_sem, c_send, c_recv, x_send, x_recv, own_sem, f_send, f_recv, t_send, t_recv,
):
    n0, n1, n2 = cfg["dims"]
    lags, n_chunks, n_small = cfg["lags"], cfg["chunks"], cfg["small"]
    n_steps, slots = len(lags) - 1, acc.shape[0]
    dp, sub = lax.axis_index("dp"), lax.axis_index("sub")
    q2, q1, q0 = dp % n2, (dp // n2) % n1, dp // (n2 * n1)

    def chip(a, b, c):
        return (a * (n1 * n2) + b * n2 + c, sub)

    peers = [lambda v: chip(v, q1, q2), lambda v: chip(q0, v, q2), lambda v: chip(q0, q1, v)]
    places = list(zip((n0, n1, n2), (q0, q1, q2), peers, strict=True))
    l0, l1, l2 = (Line(n, q, peer) for n, q, peer in places)
    core = (dp, 1 - sub)
    part_rows = CHUNK // 4
    parts = [Part([l2, l0, l1], part_rows), Part([l1, l0, l2], part_rows)]
    n_rs = parts[0].n_rs
    tokens, width = nm.shape
    chosen = bias.shape[1]
    rows = tokens // chosen
    pieces = w_up_h.shape[1] // PIECE

    loads = [
        pltpu.make_async_copy(src, dst, load_sem.at[i])
        for i, (src, dst) in enumerate(
            (
                (nm_h, nm), (dmix_h, dmix), (qkv_h, qkv), (att_h, att), (cols_h, cols), (bias_h, bias),
                (picked_h, picked), (cot_h, cot), (w_qkv_h, w_qkv), (w_out_h, w_out),
            )
        )
    ]

    def weights_in(f):
        cut = pl.ds(pl.multiple_of(f * PIECE, PIECE), PIECE)
        slot = f % 2
        return (
            pltpu.make_async_copy(w_up_h.at[:, cut], w_up.at[slot], w_sem.at[slot, 0]),
            pltpu.make_async_copy(w_down_h.at[cut], w_down.at[slot], w_sem.at[slot, 1]),
        )

    def branch_in(r):
        return pltpu.make_async_copy(branch_h.at[pl.ds(r * chosen, chosen)], branch.at[r % 2], row_sem.at[r % 2])

    def normed_in():
        return pltpu.make_async_copy(normed_h, nm, load_sem.at[len(loads)])

    for i in range(2):
        loads[i].start()
    for copy in weights_in(0):
        copy.start()

    greeted = [core] + [peer((q + d) % n) for n, q, peer in places for d in range(1, n)]
    barrier = pltpu.get_barrier_semaphore()
    for device in greeted:
        pl.semaphore_signal(barrier, inc=1, device_id=device, device_id_type=MESH)
    mixed[...] = jnp.zeros_like(mixed)
    d_nm[...] = jnp.zeros_like(d_nm)
    for i in range(2):
        loads[i].wait()
    for i in range(2, len(loads)):
        loads[i].start()
    vecs[...] = jnp.zeros_like(vecs)
    for r in range(rows):
        cut = pl.ds(r * chosen, chosen)
        nm_t[:, cut] = nm[cut].T
        vecs[24:30] += colsum(dmix[cut].astype(F32))
    pl.semaphore_wait(barrier, len(greeted))


    def half_out(c):
        j = c % 3
        return pltpu.make_async_remote_copy(
            src_ref=stage.at[pl.ds(at8(j * CHUNK + (1 - sub) * (CHUNK // 2)), CHUNK // 2)], dst_ref=cbuf.at[j],
            send_sem=c_send.at[j], recv_sem=c_recv.at[j], device_id=core, device_id_type=MESH,
        )

    def out_copy(c, p, k):
        kind, ln, r, base, size, slot = parts[p].steps[k]
        who, off, n, device = (ln.rs_send if kind == "rs" else ln.ag_send)(r, size)
        here = pl.ds(at8(p * part_rows + base + off), n)
        if kind == "rs":
            src, dst = acc.at[c % slots, here], rbuf.at[c % slots, p, pl.ds(slot, n)]
        else:
            dst = sums.at[c, sub, here]
            src = acc.at[c % slots, here] if k == n_rs else dst
        return who, pltpu.make_async_remote_copy(
            src_ref=src, dst_ref=dst, send_sem=x_send.at[c % slots, p, k], recv_sem=x_recv.at[c % slots, p, k],
            device_id=device, device_id_type=MESH,
        )

    def own_copy(c, p):
        base, n = parts[p].own
        here = pl.ds(at8(p * part_rows + base), n)
        return pltpu.make_async_copy(acc.at[c % slots, here], sums.at[c, sub, here], own_sem.at[c % slots, p])

    def begin(c, p, k):
        who, copy = out_copy(c, p, k)
        when(who, copy.start)
        if k == n_rs:
            own_copy(c, p).start()

    def finish(c, p, k):
        kind, ln, r, base, size, slot = parts[p].steps[k]
        who, off, n = (ln.rs_recv if kind == "rs" else ln.ag_recv)(r, size)
        here = pl.ds(at8(p * part_rows + base + off), n)
        came = rbuf.at[c % slots, p, pl.ds(slot, n)] if kind == "rs" else sums.at[c, sub, here]

        def take():
            pltpu.make_async_remote_copy(
                src_ref=came, dst_ref=came, send_sem=x_send.at[c % slots, p, k], recv_sem=x_recv.at[c % slots, p, k],
                device_id=core, device_id_type=MESH,
            ).wait_recv()
            if kind == "rs":
                region = acc.at[c % slots, here]
                region[...] = region[...] + came[...]

        when(who, take)
        who, copy = out_copy(c, p, k)
        when(who, copy.wait_send)
        if k == n_rs:
            own_copy(c, p).wait()
        if k == n_rs - 1:
            base, n = parts[p].own
            mine = acc.at[c % slots, pl.ds(at8(p * part_rows + base), n)]
            mine[...] = mine[...] / live_s[0:1]

    def half_back(c, half):
        return pltpu.make_async_remote_copy(
            src_ref=sums.at[c, half], dst_ref=sums.at[c, half], send_sem=f_send.at[c], recv_sem=f_recv.at[c],
            device_id=core, device_id_type=MESH,
        )

    def events(t):
        for k in range(n_steps, -1, -1):
            c = t - 1 - lags[k]

            def event(k=k, c=c):
                for p in range(2):
                    if k > 0:
                        finish(c, p, k - 1)
                    elif p == 0:
                        half_out(c).wait()
                        mine = pl.ds(at8((c % 3) * CHUNK + sub * (CHUNK // 2)), CHUNK // 2)
                        acc[c % slots] = stage[mine] + cbuf[c % 3]
                    if k < n_steps:
                        begin(c, p, k)
                if k == n_steps:
                    half_back(c, sub).start()

            pl.when((c >= 0) & (c < n_chunks))(event)


    pairs = [core]
    for n, q, peer in places:
        bit = 1
        while bit < n:
            pairs.append(peer(q + bit - 2 * bit * ((q // bit) % 2)))
            bit *= 2

    def tiny_copy(which, i):
        here = pl.ds(0, 8) if which == 0 else pl.ds(8, n_small)
        return pltpu.make_async_remote_copy(
            src_ref=tiny.at[0, i, here], dst_ref=tiny.at[1, i, here],
            send_sem=t_send.at[which, i], recv_sem=t_recv.at[which, i], device_id=pairs[i], device_id_type=MESH,
        )

    def tiny_steps(t, first, which, total):
        here = pl.ds(0, 8) if which == 0 else pl.ds(8, n_small)
        for i in range(len(pairs) + 1):

            def step(i=i):
                if i > 0:
                    tiny_copy(which, i - 1).wait()
                    total[...] = total[...] + tiny[1, i - 1, here]
                if i < len(pairs):
                    tiny[0, i, here] = total[...]
                    tiny_copy(which, i).start()
                elif which == 1:
                    small_o[...] = total[...] / live_s[0:1]

            pl.when(t == first + i)(step)


    def put(base, block, value):
        for j in range(value.shape[1] // 128):
            stage[base + j * block : base + (j + 1) * block] = value[:, j * 128 : (j + 1) * 128]

    def piece_up(f):
        for copy in weights_in(f):
            copy.wait()

        def more():
            for copy in weights_in(f + 1):
                copy.start()

        pl.when(f + 1 < pieces)(more)
        slot = f % 2
        b = b_up[pl.ds(pl.multiple_of(f * PIECE, PIECE), PIECE)].astype(F32)[None]
        for r in range(rows):
            cut = pl.ds(r * chosen, chosen)
            u = nn(nm[cut], w_up[slot]) + b
            u2 = u * u
            t = jnp.tanh(GELU_A * u * (1.0 + GELU_B * u2))
            act[cut] = (0.5 * u * (1.0 + t)).astype(BF16)
            slope[cut] = 0.5 * (1.0 + t) + 0.5 * u * (1.0 - t * t) * (GELU_A * (1.0 + 3.0 * GELU_B * u2))
        put(0, PIECE, tn(act[...], dmix[...]))

    def piece_back(f):
        slot = f % 2
        sums_b = jnp.zeros((PIECE // 128, 128), F32)
        for r in range(rows):
            cut = pl.ds(r * chosen, chosen)
            d = (nt(dmix[cut], w_down[slot]) * slope[cut]).astype(BF16)
            d_up[cut] = d
            sums_b = sums_b + colsum(d.astype(F32))
        vecs[pl.ds(at8(32 + 8 * f), PIECE // 128)] = sums_b
        put(PIECE * 6, width, nn(nm_t[...], d_up[...]))

    def piece_on(f):
        slot = f % 2
        for r in range(rows):
            cut = pl.ds(r * chosen, chosen)
            mixed[cut] += nn(act[cut], w_down[slot])
            d_nm[cut] += nt(d_up[cut], w_up[slot])


    lane = lanes((chosen, 128))
    is_low = lane < HEAD

    def col(r, at):
        return cols[pl.ds(r * chosen, chosen), at : at + 1]

    def hidden_back():
        for i in range(2, len(loads)):
            loads[i].wait()
        branch_in(0).start()
        for r in range(rows):
            branch_in(r).wait()
            if r + 1 < rows:
                branch_in(r + 1).start()
            cut = pl.ds(r * chosen, chosen)
            br = branch[r % 2]
            x = picked[cut].astype(F32)
            router, live, scale = col(r, HEADS), col(r, HEADS + 1), col(r, HEADS + 3)
            hidden = x + router * br
            unit = hidden * scale
            d_res = dmix[cut].astype(F32)
            dn = d_nm[cut]
            vecs[16:22] += colsum(dn * unit)
            d_unit = dn * vector(gain_mlp)
            d_hidden = d_res + scale * (d_unit - unit * row_mean(d_unit * unit))
            dmix[cut] = (x + (hidden + mixed[cut] + vector(b_down) - x) * live).astype(BF16)
            d_router = jnp.sum(d_hidden * br, axis=-1, keepdims=True)
            vecs[0:6] += colsum(d_router * x)
            d_branch = (router * d_hidden).astype(BF16)
            nm[cut] = d_branch
            mixed[cut] = d_hidden - d_res + d_router * vector(w_router)
        pltpu.make_async_copy(dmix, new_block, out_sem.at[0]).start()
        put(0, width, tn(att[...], nm[...]))
        for r in range(rows):
            cut = pl.ds(r * chosen, chosen)
            att[cut] = nt(nm[cut], w_out[...]).astype(BF16)
        normed_in().start()

    def attention_back(r):
        cut = pl.ds(pl.multiple_of(r * chosen, chosen), chosen)
        sides = [jnp.where(side, 1.0, 0.0).astype(BF16) for side in (is_low, ~is_low)]
        for pair in range(HEADS // 2):
            sq, sk, sv = (pl.ds(i * width + pair * 128, 128) for i in range(3))
            q, k, v, do = qkv[cut, sq], qkv[cut, sk], qkv[cut, sv], att[cut, sq]
            scores = [nt(q * side, k) for side in sides]
            d_values = [nt(do * side, v) for side in sides]
            made = []
            for a in range(2):
                log_total = cols[cut, 2 * pair + a : 2 * pair + a + 1]
                probs = jnp.exp(scores[a] * HEAD**-0.5 + bias[cut].astype(F32) - log_total)
                d_probs = d_values[a]
                d_scores = probs * (d_probs - jnp.sum(d_probs * probs, axis=-1, keepdims=True))
                d_scores = d_scores.astype(BF16)
                made.append((nn(d_scores, k), tn(d_scores, q), tn(probs.astype(BF16), do)))
            dq, dk, dv = (jnp.where(is_low, x, y) for x, y in zip(*made, strict=True))
            qkv[cut, sq] = (dq * HEAD**-0.5).astype(BF16)
            qkv[cut, sk] = (dk * HEAD**-0.5).astype(BF16)
            qkv[cut, sv] = dv.astype(BF16)

    def tokens_back(r):
        cut = pl.ds(r * chosen, chosen)
        d_normed = nt(qkv[cut], w_qkv[...])
        x = picked[cut].astype(F32)
        scale = col(r, HEADS + 2)
        unit = x * scale
        vecs[8:14] += colsum(d_normed * unit)
        d_unit = d_normed * vector(gain_attn)
        d_picked = mixed[cut] + scale * (d_unit - unit * row_mean(d_unit * unit))
        cot[cut] = (cot[cut].astype(F32) + d_picked).astype(BF16)

    def compute(t):
        @pl.when(t < 3 * pieces)
        def _():
            f = t // 3
            pl.when(t % 3 == 0)(lambda: piece_up(f))
            pl.when(t % 3 == 1)(lambda: piece_back(f))
            pl.when(t % 3 == 2)(lambda: piece_on(f))

        t0 = 3 * pieces
        pl.when(t == t0)(hidden_back)

        @pl.when(t == t0 + 1)
        def _():
            lax.fori_loop(0, rows // 2, lambda r, i: (attention_back(r), i)[1], 0)

        @pl.when(t == t0 + 2)
        def _():
            lax.fori_loop(rows // 2, rows, lambda r, i: (attention_back(r), i)[1], 0)
            normed_in().wait()
            put(6 * width, width, tn(nm[...], qkv[:, 0:256]))

        @pl.when(t == t0 + 3)
        def _():
            put(0, width, tn(nm[...], qkv[:, 256:1280]))

        @pl.when(t == t0 + 6)
        def _():
            put(0, width, tn(nm[...], qkv[:, 1280:2304]))

        @pl.when(t == t0 + 8)
        def _():
            for r in range(rows):
                tokens_back(r)
            pltpu.make_async_copy(cot, new_grad, out_sem.at[1]).start()

    live_s[...] = live_in[...]

    def tick(t, carry):
        events(t)
        compute(t)
        pl.when(t < n_chunks)(lambda: half_out(t).start())
        tiny_steps(t, 0, 0, live_s)
        tiny_steps(t, n_chunks, 1, vecs)
        return carry

    lax.fori_loop(0, n_chunks + lags[-1] + 1, tick, 0)

    def last(c, carry):
        half_back(c, sub).wait_send()
        half_back(c, 1 - sub).wait_recv()
        return carry

    lax.fori_loop(0, n_chunks, last, 0)
    pltpu.make_async_copy(dmix, new_block, out_sem.at[0]).wait()
    pltpu.make_async_copy(cot, new_grad, out_sem.at[1]).wait()


def device_sums(mesh, made, weights, vectors):
    picked, cot, dmix, normed, qkv, att, cols, bias, branch, nm, live = made
    w_qkv, w_out, w_up, w_down = weights
    tokens, width = nm.shape
    chosen = bias.shape[1]
    hidden = w_up.shape[1]
    dims = {16: (4, 2, 2), 64: (4, 4, 4)}[mesh.shape["dp"]]
    n_steps = 2 * sum(ROUNDS[n] for n in dims)
    lags = lags_of(n_steps)
    slots = lags[n_steps // 2 + 1] + 1
    chunks = (2 * width * hidden + width * width * 4) // (128 * CHUNK)
    part_rows = CHUNK // 4
    came = max(recv_rows(order, part_rows) for order in ((dims[2], dims[0], dims[1]), (dims[1], dims[0], dims[2])))
    n_tiny = 1 + sum({1: 0, 2: 1, 4: 2}[n] for n in dims)
    n_small = 32 + 8 * (hidden // PIECE)
    vmem, dma = pltpu.VMEM, pltpu.SemaphoreType.DMA
    big = pl.BlockSpec(memory_space=pl.ANY)
    near = pl.BlockSpec(memory_space=vmem)
    return pl.pallas_call(
        functools.partial(sums_kernel, dict(dims=dims, lags=lags, chunks=chunks, small=n_small)),
        in_specs=[big] * 14 + [near] * 6,
        out_specs=[big, near, big, big],
        out_shape=[
            jax.ShapeDtypeStruct((chunks, 2, CHUNK // 2, 128), F32),
            jax.ShapeDtypeStruct((n_small, 128), F32),
            jax.ShapeDtypeStruct((tokens, width), BF16),
            jax.ShapeDtypeStruct((tokens, width), BF16),
        ],
        scratch_shapes=[
            vmem((tokens, width), BF16),
            vmem((width, tokens), BF16),
            vmem((tokens, width), BF16),
            vmem((2, width, PIECE), BF16),
            vmem((2, PIECE, width), BF16),
            vmem((tokens, PIECE), BF16),
            vmem((tokens, PIECE), F32),
            vmem((tokens, PIECE), BF16),
            vmem((tokens, width), F32),
            vmem((tokens, width), F32),
            vmem((tokens, 3 * width), BF16),
            vmem((tokens, width), BF16),
            vmem((tokens, 128), F32),
            vmem((tokens, chosen), BF16),
            vmem((2, chosen, width), F32),
            vmem((tokens, width), BF16),
            vmem((tokens, width), BF16),
            vmem((width, 3 * width), BF16),
            vmem((width, width), BF16),
            vmem((3 * CHUNK, 128), F32),
            vmem((3, CHUNK // 2, 128), F32),
            vmem((slots, CHUNK // 2, 128), F32),
            vmem((slots, 2, came, 128), F32),
            vmem((n_small, 128), F32),
            vmem((8, 128), F32),
            vmem((2, n_tiny, n_small + 8, 128), F32),
            dma((11,)),
            dma((2, 2)),
            dma((2,)),
            dma((2,)),
            dma((3,)),
            dma((3,)),
            dma((slots, 2, n_steps)),
            dma((slots, 2, n_steps)),
            dma((slots, 2)),
            dma((chunks,)),
            dma((chunks,)),
            dma((2, n_tiny)),
            dma((2, n_tiny)),
        ],
        compiler_params=pltpu.CompilerParams(collective_id=0, has_side_effects=True, vmem_limit_bytes=63 * 2**20),
    )(nm, dmix, normed, qkv, att, cols, bias, branch, picked, cot, w_up, w_down, w_qkv, w_out, live, *vectors)


def last_kernel(
    selected, tokens, cot, new_block, new_grad, sums,
    block_out, grad_tokens, grad_qkv, grad_out, grad_up, grad_down, near, in_sems, sems,
):
    step = pl.program_id(0) * pl.num_programs(1) + pl.program_id(1)
    width, hidden = grad_up.shape
    copies = []

    def copy(row, n, dst):
        copies.append((row // GROUP, pltpu.make_async_copy(near.at[pl.ds(row, n)], dst, sems.at[len(copies)])))
        return row + n

    row = 0
    for f in range(0, hidden, PIECE):
        for j in range(0, width, 128):
            row = copy(row, PIECE, grad_down.at[pl.ds(f, PIECE), pl.ds(j, 128)])
        for j in range(f, f + PIECE, 128):
            row = copy(row, width, grad_up.at[:, pl.ds(j, 128)])
    for j in range(0, width, 128):
        row = copy(row, width, grad_out.at[:, pl.ds(j, 128)])
    for j in range(0, 3 * width, 128):
        row = copy(row, width, grad_qkv.at[:, pl.ds(j, 128)])

    groups = sums.shape[0] // GROUP
    fetch = [
        pltpu.make_async_copy(sums.at[pl.ds(g * GROUP, GROUP)], near.at[pl.ds(g * GROUP, GROUP)], in_sems.at[g])
        for g in range(groups)
    ]
    steps = pl.num_programs(0) * pl.num_programs(1)

    @pl.when(step == 0)
    def _():
        for f in fetch:
            f.start()

    for g in range(groups):

        @pl.when(step == jnp.minimum(g, steps - 1))
        def _(g=g):
            fetch[g].wait()
            for at, c in copies:
                if at == g:
                    c.start()

    spots = tokens.shape[1]
    sel = selected[pl.ds(pl.program_id(0), 1)]
    spot = lax.broadcasted_iota(jnp.int32, (spots, sel.shape[1]), 0) + pl.program_id(1) * spots
    hot = jnp.where(spot == sel, 1.0, 0.0)
    hit = jnp.max(hot, axis=-1, keepdims=True) > 0.0
    hot = hot.astype(BF16)
    for old, new, out in ((tokens, new_block, block_out), (cot, new_grad, grad_tokens)):
        fresh = nn(hot, new[...])
        out[0] = jnp.where(hit, fresh, old[0].astype(F32)).astype(BF16)

    @pl.when(step == steps - 1)
    def _():
        for _, c in copies:
            c.wait()


def last(tokens, cotangent, selected, new_block, new_grad, sums, hidden):
    rows, spots, width = tokens.shape
    chosen = selected.shape[1]
    cut = 1024
    big = pl.BlockSpec(memory_space=pl.ANY)
    table = pl.BlockSpec((1, cut, width), lambda r, i: (r, i, 0))
    fresh = pl.BlockSpec((chosen, width), lambda r, i: (r, 0))
    n_copies = hidden // PIECE * (width // 128) + hidden // 128 + 4 * (width // 128)
    return pl.pallas_call(
        last_kernel,
        grid=(rows, spots // cut),
        in_specs=[pl.BlockSpec(selected.shape, lambda r, i: (0, 0)), table, table, fresh, fresh, big],
        out_specs=[table, table, big, big, big, big],
        out_shape=[
            jax.ShapeDtypeStruct(tokens.shape, BF16),
            jax.ShapeDtypeStruct(tokens.shape, BF16),
            jax.ShapeDtypeStruct((width, 3 * width), F32),
            jax.ShapeDtypeStruct((width, width), F32),
            jax.ShapeDtypeStruct((width, hidden), F32),
            jax.ShapeDtypeStruct((hidden, width), F32),
        ],
        scratch_shapes=[
            pltpu.VMEM(sums.shape, F32),
            pltpu.SemaphoreType.DMA((sums.shape[0] // GROUP,)),
            pltpu.SemaphoreType.DMA((n_copies,)),
        ],
        compiler_params=pltpu.CompilerParams(vmem_limit_bytes=63 * 2**20),
    )(selected, tokens, cotangent, new_block, new_grad, sums)


def body(
    mesh, tokens, doc_lengths, selected, w_router, gain_attn, w_qkv, w_out, gain_mlp, w_up, b_up, w_down, b_down, cotangent
):
    hidden = w_up.shape[1]
    made = first(tokens, doc_lengths, selected, cotangent, w_router, gain_attn, w_qkv, w_out, gain_mlp)
    sums, small, new_block, new_grad = device_sums(
        mesh, made, (w_qkv, w_out, w_up, w_down), (b_up, b_down, w_router, gain_attn, gain_mlp)
    )
    block_out, grad_tokens, grad_qkv, grad_out, grad_up, grad_down = last(
        tokens, cotangent, selected, new_block, new_grad, sums.reshape(-1, 128), hidden
    )
    grad_b_up = small[32:].reshape(-1, 8, 128)[:, : PIECE // 128].reshape(-1)
    grad_router, grad_gain_attn, grad_gain_mlp, grad_b_down = (small[i : i + 6].reshape(-1) for i in (0, 8, 16, 24))
    return (
        block_out,
        grad_tokens,
        grad_router,
        grad_gain_attn,
        grad_qkv,
        grad_out,
        grad_gain_mlp,
        grad_up,
        grad_b_up,
        grad_down,
        grad_b_down,
    )


def solution(mesh):
    split, copied = P(("dp", "sub")), P()
    return jax.shard_map(
        functools.partial(body, mesh),
        mesh=mesh,
        in_specs=(split,) * 3 + (copied,) * 9 + (split,),
        out_specs=(split,) * 2 + (copied,) * 9,
        check_vma=False,
    )
```

```python
import functools

import jax
import jax.numpy as jnp
from jax import lax
from jax.experimental import pallas as pl
from jax.experimental.pallas import tpu as pltpu
from jax.sharding import PartitionSpec as P

HEADS = 12
HEAD = 64
EPS = 1e-06
CHUNK = 2048
GROUP = 3 * CHUNK
PIECE = 512
BIG = -1e30
GELU_A = 0.7978845608028654
GELU_B = 0.044715
ROUNDS = {1: 0, 2: 1, 4: 3}
MESH = pl.DeviceIdType.MESH
F32 = jnp.float32
BF16 = jnp.bfloat16


def nn(a, b):
    return lax.dot_general(a, b, (((1,), (0,)), ((), ())), preferred_element_type=F32)


def nt(a, b):
    return lax.dot_general(a, b, (((1,), (1,)), ((), ())), preferred_element_type=F32)


def tn(a, b):
    return lax.dot_general(a, b, (((0,), (0,)), ((), ())), preferred_element_type=F32)


def vector(ref):
    return ref[...].astype(F32)[None]


def lanes(shape):
    return lax.broadcasted_iota(jnp.int32, shape, len(shape) - 1)


def row_mean(v):
    return jnp.mean(v, axis=-1, keepdims=True)


def colsum(v):
    total = jnp.sum(v, axis=0, keepdims=True)
    return jnp.concatenate([total[:, j : j + 128] for j in range(0, v.shape[1], 128)], axis=0)


def when(cond, act):
    if cond is None:
        act()
    else:
        pl.when(cond)(act)


def at8(v):
    return v if isinstance(v, int) else pl.multiple_of(v, 8)


def first_kernel(
    lens, selected, tokens, cot, w_router, gain_attn, w_qkv, w_out, gain_mlp,
    picked_o, cot_o, dmix_o, normed_o, qkv_o, att_o, cols_o, bias_o, branch_o, nm_o, live_o,
):
    r = pl.program_id(0)
    chosen = selected.shape[1]
    selr = selected[pl.ds(r, 1)]
    diagonal = lanes((chosen, chosen)) == lax.broadcasted_iota(jnp.int32, (chosen, chosen), 0)
    sel = jnp.sum(jnp.where(diagonal, selr.astype(F32), 0.0), axis=-1, keepdims=True).astype(jnp.int32)
    end = jnp.int32(0)
    seg = jnp.zeros(sel.shape, jnp.int32)
    segr = jnp.zeros(selr.shape, jnp.int32)
    for d in range(lens.shape[1]):
        end = end + lens[r, d]
        seg = seg + (sel >= end).astype(jnp.int32)
        segr = segr + (selr >= end).astype(jnp.int32)
    live = (sel < end).astype(F32)
    count = jnp.broadcast_to(jnp.sum(live), live_o.shape)

    @pl.when(r == 0)
    def _():
        live_o[...] = count

    @pl.when(r > 0)
    def _():
        live_o[...] += count

    spots = tokens.shape[1]
    hot = jnp.where(lanes((chosen, spots)) == sel, 1.0, 0.0).astype(BF16)
    picked = nn(hot, tokens[0])
    cot_rows = nn(hot, cot[0])
    picked_o[...] = picked.astype(BF16)
    cot_o[...] = cot_rows.astype(BF16)
    dmix_o[...] = (cot_rows * live).astype(BF16)
    router = jnp.sum(picked * vector(w_router), axis=-1, keepdims=True)
    scale_attn = lax.rsqrt(row_mean(picked * picked) + EPS)
    normed = (picked * scale_attn * vector(gain_attn)).astype(BF16)
    normed_o[...] = normed
    qkv_o[...] = nn(normed, w_qkv[...]).astype(BF16)
    width = picked.shape[1]
    causal = lanes((chosen, chosen)) <= lax.broadcasted_iota(jnp.int32, (chosen, chosen), 0)
    bias_o[...] = jnp.where(causal & (seg == segr), 0.0, BIG).astype(BF16)
    lane = lanes((chosen, 128))
    is_low = lane < HEAD
    cols = jnp.zeros((chosen, 128), F32)
    for pair in range(HEADS // 2):
        q = qkv_o[:, pair * 128 : pair * 128 + 128]
        k = qkv_o[:, width + pair * 128 : width + pair * 128 + 128]
        v = qkv_o[:, 2 * width + pair * 128 : 2 * width + pair * 128 + 128]
        outs = []
        for a in range(2):
            keep = jnp.where(is_low if a == 0 else ~is_low, HEAD**-0.5, 0.0).astype(BF16)
            scores = nt(q * keep, k) + bias_o[...].astype(F32)
            top = jnp.max(scores, axis=-1, keepdims=True)
            exponent = jnp.exp(scores - top)
            total = jnp.sum(exponent, axis=-1, keepdims=True)
            outs.append(nn((exponent * (1.0 / total)).astype(BF16), v))
            cols = jnp.where(lane == 2 * pair + a, top + jnp.log(total), cols)
        att_o[:, pair * 128 : pair * 128 + 128] = jnp.where(is_low, outs[0], outs[1]).astype(BF16)
    branch = nn(att_o[...], w_out[...])
    branch_o[...] = branch
    hidden = picked + router * branch
    scale_mlp = lax.rsqrt(row_mean(hidden * hidden) + EPS)
    nm_o[...] = (hidden * scale_mlp * vector(gain_mlp)).astype(BF16)
    for at, col in enumerate((router, live, scale_attn, scale_mlp)):
        cols = jnp.where(lane == HEADS + at, col, cols)
    cols_o[...] = cols


def first(tokens, doc_lengths, selected, cotangent, w_router, gain_attn, w_qkv, w_out, gain_mlp):
    rows, spots, width = tokens.shape
    chosen = selected.shape[1]
    n = rows * chosen

    def whole(a):
        return pl.BlockSpec(a.shape, lambda r: (0,) * a.ndim)

    def out(cols, kind):
        return jax.ShapeDtypeStruct((n, cols), kind), pl.BlockSpec((chosen, cols), lambda r: (r, 0))

    outs = [
        out(width, BF16), out(width, BF16), out(width, BF16), out(width, BF16), out(3 * width, BF16),
        out(width, BF16), out(128, F32), out(chosen, BF16), out(width, F32), out(width, BF16),
        (jax.ShapeDtypeStruct((8, 128), F32), pl.BlockSpec((8, 128), lambda r: (0, 0))),
    ]
    return pl.pallas_call(
        first_kernel,
        grid=(rows,),
        in_specs=[
            pl.BlockSpec(memory_space=pltpu.SMEM),
            whole(selected),
            pl.BlockSpec((1, spots, width), lambda r: (r, 0, 0)),
            pl.BlockSpec((1, spots, width), lambda r: (r, 0, 0)),
            whole(w_router), whole(gain_attn), whole(w_qkv), whole(w_out), whole(gain_mlp),
        ],
        out_specs=[o[1] for o in outs],
        out_shape=[o[0] for o in outs],
        compiler_params=pltpu.CompilerParams(vmem_limit_bytes=63 * 2**20),
    )(
        doc_lengths, selected, tokens, cotangent,
        w_router, gain_attn, w_qkv, w_out, gain_mlp,
    )


class Line:
    def __init__(self, n, q, peer):
        self.n, self.q, self.peer = n, q, peer
        self.rounds = ROUNDS[n]
        if n == 4:
            self.side = q // 2
            self.inner = (q == 1) | (q == 2)
            self.outer = jnp.logical_not(self.inner)

    def rs_send(self, r, size):
        h, s = size // self.n, self.q if self.n == 2 else getattr(self, "side", 0)
        if self.n == 2:
            return None, (1 - s) * h, h, self.peer(1 - s)
        if r == 0:
            return self.outer, (1 - s) * h, 3 * h, self.peer(1 + s)
        if r == 1:
            return self.inner, (1 - s) * 2 * h, 2 * h, self.peer(2 - s)
        return self.inner, s * 3 * h, h, self.peer(3 * s)

    def rs_recv(self, r, size):
        h, s = size // self.n, self.q if self.n == 2 else getattr(self, "side", 0)
        if self.n == 2:
            return None, s * h, h
        if r == 0:
            return self.inner, (1 - s) * h, 3 * h
        if r == 1:
            return self.inner, s * 2 * h, 2 * h
        return self.outer, s * 3 * h, h

    def ag_send(self, r, size):
        h, s = size // self.n, self.q if self.n == 2 else getattr(self, "side", 0)
        if self.n == 2:
            return None, s * h, h, self.peer(1 - s)
        if r == 0:
            return self.outer, s * 3 * h, h, self.peer(1 + s)
        if r == 1:
            return self.inner, s * 2 * h, 2 * h, self.peer(2 - s)
        return self.inner, (1 - s) * h, 3 * h, self.peer(3 * s)

    def ag_recv(self, r, size):
        h, s = size // self.n, self.q if self.n == 2 else getattr(self, "side", 0)
        if self.n == 2:
            return None, (1 - s) * h, h
        if r == 0:
            return self.inner, s * 3 * h, h
        if r == 1:
            return self.inner, (1 - s) * 2 * h, 2 * h
        return self.outer, (1 - s) * h, 3 * h


def recv_rows(sizes, rows):
    total = 0
    for n in sizes:
        rows = rows // n
        total += {1: 0, 2: 1, 4: 5}[n] * rows
    return total


class Part:
    def __init__(self, lines, rows):
        self.steps = []
        base, size, slot = 0, rows, 0
        levels = []
        for ln in lines:
            h = size // ln.n
            offs = {1: [], 2: [slot], 4: [slot, slot + 3 * h, slot]}[ln.n]
            slot += {1: 0, 2: 1, 4: 5}[ln.n] * h
            levels.append((ln, base, size))
            for r in range(ln.rounds):
                self.steps.append(("rs", ln, r, base, size, offs[r]))
            if ln.n > 1:
                base = base + ln.q * h
            size = h
        self.own = (base, size)
        self.n_rs = len(self.steps)
        for ln, b, s in reversed(levels):
            for r in range(ln.rounds):
                self.steps.append(("ag", ln, r, b, s, None))


def lags_of(n_steps):
    lags = [0]
    for k in range(n_steps):
        lags.append(lags[-1] + (2 if k < 2 or k >= n_steps - 2 else 1))
    return lags


def sums_kernel(
    cfg,
    nm_h, dmix_h, normed_h, qkv_h, att_h, cols_h, bias_h, branch_h, picked_h, cot_h, w_up_h, w_down_h, w_qkv_h, w_out_h,
    live_in, b_up, b_down, w_router, gain_attn, gain_mlp,
    sums, small_o, new_block, new_grad,
    nm, nm_t, dmix, w_up, w_down, act, slope, d_up, mixed, d_nm, qkv, att, cols, bias, branch, picked, cot, w_qkv, w_out,
    stage, cbuf, acc, rbuf, vecs, live_s, tiny,
    load_sem, w_sem, row_sem, out_sem, c_send, c_recv, x_send, x_recv, own_sem, f_send, f_recv, t_send, t_recv,
):
    n0, n1, n2 = cfg["dims"]
    lags, n_chunks, n_small = cfg["lags"], cfg["chunks"], cfg["small"]
    n_steps, slots = len(lags) - 1, acc.shape[0]
    dp, sub = lax.axis_index("dp"), lax.axis_index("sub")
    q2, q1, q0 = dp % n2, (dp // n2) % n1, dp // (n2 * n1)

    def chip(a, b, c):
        return (a * (n1 * n2) + b * n2 + c, sub)

    peers = [lambda v: chip(v, q1, q2), lambda v: chip(q0, v, q2), lambda v: chip(q0, q1, v)]
    places = list(zip((n0, n1, n2), (q0, q1, q2), peers, strict=True))
    l0, l1, l2 = (Line(n, q, peer) for n, q, peer in places)
    core = (dp, 1 - sub)
    part_rows = CHUNK // 4
    parts = [Part([l2, l0, l1], part_rows), Part([l1, l0, l2], part_rows)]
    n_rs = parts[0].n_rs
    tokens, width = nm.shape
    chosen = bias.shape[1]
    rows = tokens // chosen
    pieces = w_up_h.shape[1] // PIECE

    loads = [
        pltpu.make_async_copy(src, dst, load_sem.at[i])
        for i, (src, dst) in enumerate(
            (
                (nm_h, nm), (dmix_h, dmix), (qkv_h, qkv), (att_h, att), (cols_h, cols), (bias_h, bias),
                (picked_h, picked), (cot_h, cot), (w_qkv_h, w_qkv), (w_out_h, w_out),
            )
        )
    ]

    def weights_in(f):
        cut = pl.ds(pl.multiple_of(f * PIECE, PIECE), PIECE)
        slot = f % 2
        return (
            pltpu.make_async_copy(w_up_h.at[:, cut], w_up.at[slot], w_sem.at[slot, 0]),
            pltpu.make_async_copy(w_down_h.at[cut], w_down.at[slot], w_sem.at[slot, 1]),
        )

    def branch_in(r):
        return pltpu.make_async_copy(branch_h.at[pl.ds(r * chosen, chosen)], branch.at[r % 2], row_sem.at[r % 2])

    def normed_in():
        return pltpu.make_async_copy(normed_h, nm, load_sem.at[len(loads)])

    for i in range(2):
        loads[i].start()
    for copy in weights_in(0):
        copy.start()

    greeted = [core] + [peer((q + d) % n) for n, q, peer in places for d in range(1, n)]
    barrier = pltpu.get_barrier_semaphore()
    for device in greeted:
        pl.semaphore_signal(barrier, inc=1, device_id=device, device_id_type=MESH)
    mixed[...] = jnp.zeros_like(mixed)
    d_nm[...] = jnp.zeros_like(d_nm)
    for i in range(2):
        loads[i].wait()
    for i in range(2, len(loads)):
        loads[i].start()
    vecs[...] = jnp.zeros_like(vecs)
    for r in range(rows):
        cut = pl.ds(r * chosen, chosen)
        nm_t[:, cut] = nm[cut].T
        vecs[24:30] += colsum(dmix[cut].astype(F32))
    pl.semaphore_wait(barrier, len(greeted))


    def half_out(c):
        j = c % 3
        return pltpu.make_async_remote_copy(
            src_ref=stage.at[pl.ds(at8(j * CHUNK + (1 - sub) * (CHUNK // 2)), CHUNK // 2)], dst_ref=cbuf.at[j],
            send_sem=c_send.at[j], recv_sem=c_recv.at[j], device_id=core, device_id_type=MESH,
        )

    def out_copy(c, p, k):
        kind, ln, r, base, size, slot = parts[p].steps[k]
        who, off, n, device = (ln.rs_send if kind == "rs" else ln.ag_send)(r, size)
        here = pl.ds(at8(p * part_rows + base + off), n)
        if kind == "rs":
            src, dst = acc.at[c % slots, here], rbuf.at[c % slots, p, pl.ds(slot, n)]
        else:
            dst = sums.at[c, sub, here]
            src = acc.at[c % slots, here] if k == n_rs else dst
        return who, pltpu.make_async_remote_copy(
            src_ref=src, dst_ref=dst, send_sem=x_send.at[c % slots, p, k], recv_sem=x_recv.at[c % slots, p, k],
            device_id=device, device_id_type=MESH,
        )

    def own_copy(c, p):
        base, n = parts[p].own
        here = pl.ds(at8(p * part_rows + base), n)
        return pltpu.make_async_copy(acc.at[c % slots, here], sums.at[c, sub, here], own_sem.at[c % slots, p])

    def begin(c, p, k):
        who, copy = out_copy(c, p, k)
        when(who, copy.start)
        if k == n_rs:
            own_copy(c, p).start()

    def finish(c, p, k):
        kind, ln, r, base, size, slot = parts[p].steps[k]
        who, off, n = (ln.rs_recv if kind == "rs" else ln.ag_recv)(r, size)
        here = pl.ds(at8(p * part_rows + base + off), n)
        came = rbuf.at[c % slots, p, pl.ds(slot, n)] if kind == "rs" else sums.at[c, sub, here]

        def take():
            pltpu.make_async_remote_copy(
                src_ref=came, dst_ref=came, send_sem=x_send.at[c % slots, p, k], recv_sem=x_recv.at[c % slots, p, k],
                device_id=core, device_id_type=MESH,
            ).wait_recv()
            if kind == "rs":
                region = acc.at[c % slots, here]
                region[...] = region[...] + came[...]

        when(who, take)
        who, copy = out_copy(c, p, k)
        when(who, copy.wait_send)
        if k == n_rs:
            own_copy(c, p).wait()
        if k == n_rs - 1:
            base, n = parts[p].own
            mine = acc.at[c % slots, pl.ds(at8(p * part_rows + base), n)]
            mine[...] = mine[...] / live_s[0:1]

    def half_back(c, half):
        return pltpu.make_async_remote_copy(
            src_ref=sums.at[c, half], dst_ref=sums.at[c, half], send_sem=f_send.at[c], recv_sem=f_recv.at[c],
            device_id=core, device_id_type=MESH,
        )

    def events(t):
        for k in range(n_steps, -1, -1):
            c = t - 1 - lags[k]

            def event(k=k, c=c):
                for p in range(2):
                    if k > 0:
                        finish(c, p, k - 1)
                    elif p == 0:
                        half_out(c).wait()
                        mine = pl.ds(at8((c % 3) * CHUNK + sub * (CHUNK // 2)), CHUNK // 2)
                        acc[c % slots] = stage[mine] + cbuf[c % 3]
                    if k < n_steps:
                        begin(c, p, k)
                if k == n_steps:
                    half_back(c, sub).start()

            pl.when((c >= 0) & (c < n_chunks))(event)


    pairs = [core]
    for n, q, peer in places:
        bit = 1
        while bit < n:
            pairs.append(peer(q + bit - 2 * bit * ((q // bit) % 2)))
            bit *= 2

    def tiny_copy(which, i):
        here = pl.ds(0, 8) if which == 0 else pl.ds(8, n_small)
        return pltpu.make_async_remote_copy(
            src_ref=tiny.at[0, i, here], dst_ref=tiny.at[1, i, here],
            send_sem=t_send.at[which, i], recv_sem=t_recv.at[which, i], device_id=pairs[i], device_id_type=MESH,
        )

    def tiny_steps(t, first, which, total):
        here = pl.ds(0, 8) if which == 0 else pl.ds(8, n_small)
        for i in range(len(pairs) + 1):

            def step(i=i):
                if i > 0:
                    tiny_copy(which, i - 1).wait()
                    total[...] = total[...] + tiny[1, i - 1, here]
                if i < len(pairs):
                    tiny[0, i, here] = total[...]
                    tiny_copy(which, i).start()
                elif which == 1:
                    small_o[...] = total[...] / live_s[0:1]

            pl.when(t == first + i)(step)


    def put(base, block, value):
        for j in range(value.shape[1] // 128):
            stage[base + j * block : base + (j + 1) * block] = value[:, j * 128 : (j + 1) * 128]

    def piece_up(f):
        for copy in weights_in(f):
            copy.wait()

        def more():
            for copy in weights_in(f + 1):
                copy.start()

        pl.when(f + 1 < pieces)(more)
        slot = f % 2
        b = b_up[pl.ds(pl.multiple_of(f * PIECE, PIECE), PIECE)].astype(F32)[None]
        for r in range(rows):
            cut = pl.ds(r * chosen, chosen)
            u = nn(nm[cut], w_up[slot]) + b
            u2 = u * u
            t = jnp.tanh(GELU_A * u * (1.0 + GELU_B * u2))
            act[cut] = (0.5 * u * (1.0 + t)).astype(BF16)
            slope[cut] = 0.5 * (1.0 + t) + 0.5 * u * (1.0 - t * t) * (GELU_A * (1.0 + 3.0 * GELU_B * u2))
        put(0, PIECE, tn(act[...], dmix[...]))

    def piece_back(f):
        slot = f % 2
        sums_b = jnp.zeros((PIECE // 128, 128), F32)
        for r in range(rows):
            cut = pl.ds(r * chosen, chosen)
            d = (nt(dmix[cut], w_down[slot]) * slope[cut]).astype(BF16)
            d_up[cut] = d
            sums_b = sums_b + colsum(d.astype(F32))
        vecs[pl.ds(at8(32 + 8 * f), PIECE // 128)] = sums_b
        put(PIECE * 6, width, nn(nm_t[...], d_up[...]))

    def piece_on(f):
        slot = f % 2
        for r in range(rows):
            cut = pl.ds(r * chosen, chosen)
            mixed[cut] += nn(act[cut], w_down[slot])
            d_nm[cut] += nt(d_up[cut], w_up[slot])


    lane = lanes((chosen, 128))
    is_low = lane < HEAD

    def col(r, at):
        return cols[pl.ds(r * chosen, chosen), at : at + 1]

    def hidden_back():
        for i in range(2, len(loads)):
            loads[i].wait()
        branch_in(0).start()
        for r in range(rows):
            branch_in(r).wait()
            if r + 1 < rows:
                branch_in(r + 1).start()
            cut = pl.ds(r * chosen, chosen)
            br = branch[r % 2]
            x = picked[cut].astype(F32)
            router, live, scale = col(r, HEADS), col(r, HEADS + 1), col(r, HEADS + 3)
            hidden = x + router * br
            unit = hidden * scale
            d_res = dmix[cut].astype(F32)
            dn = d_nm[cut]
            vecs[16:22] += colsum(dn * unit)
            d_unit = dn * vector(gain_mlp)
            d_hidden = d_res + scale * (d_unit - unit * row_mean(d_unit * unit))
            dmix[cut] = (x + (hidden + mixed[cut] + vector(b_down) - x) * live).astype(BF16)
            d_router = jnp.sum(d_hidden * br, axis=-1, keepdims=True)
            vecs[0:6] += colsum(d_router * x)
            d_branch = (router * d_hidden).astype(BF16)
            nm[cut] = d_branch
            mixed[cut] = d_hidden - d_res + d_router * vector(w_router)
        pltpu.make_async_copy(dmix, new_block, out_sem.at[0]).start()
        put(0, width, tn(att[...], nm[...]))
        for r in range(rows):
            cut = pl.ds(r * chosen, chosen)
            att[cut] = nt(nm[cut], w_out[...]).astype(BF16)
        normed_in().start()

    def attention_back(r):
        cut = pl.ds(pl.multiple_of(r * chosen, chosen), chosen)
        sides = [jnp.where(side, 1.0, 0.0).astype(BF16) for side in (is_low, ~is_low)]
        for pair in range(HEADS // 2):
            sq, sk, sv = (pl.ds(i * width + pair * 128, 128) for i in range(3))
            q, k, v, do = qkv[cut, sq], qkv[cut, sk], qkv[cut, sv], att[cut, sq]
            scores = [nt(q * side, k) for side in sides]
            d_values = [nt(do * side, v) for side in sides]
            made = []
            for a in range(2):
                log_total = cols[cut, 2 * pair + a : 2 * pair + a + 1]
                probs = jnp.exp(scores[a] * HEAD**-0.5 + bias[cut].astype(F32) - log_total)
                d_probs = d_values[a]
                d_scores = probs * (d_probs - jnp.sum(d_probs * probs, axis=-1, keepdims=True))
                d_scores = d_scores.astype(BF16)
                made.append((nn(d_scores, k), tn(d_scores, q), tn(probs.astype(BF16), do)))
            dq, dk, dv = (jnp.where(is_low, x, y) for x, y in zip(*made, strict=True))
            qkv[cut, sq] = (dq * HEAD**-0.5).astype(BF16)
            qkv[cut, sk] = (dk * HEAD**-0.5).astype(BF16)
            qkv[cut, sv] = dv.astype(BF16)

    def tokens_back(r):
        cut = pl.ds(r * chosen, chosen)
        d_normed = nt(qkv[cut], w_qkv[...])
        x = picked[cut].astype(F32)
        scale = col(r, HEADS + 2)
        unit = x * scale
        vecs[8:14] += colsum(d_normed * unit)
        d_unit = d_normed * vector(gain_attn)
        d_picked = mixed[cut] + scale * (d_unit - unit * row_mean(d_unit * unit))
        cot[cut] = (cot[cut].astype(F32) + d_picked).astype(BF16)

    def compute(t):
        @pl.when(t < 3 * pieces)
        def _():
            f = t // 3
            pl.when(t % 3 == 0)(lambda: piece_up(f))
            pl.when(t % 3 == 1)(lambda: piece_back(f))
            pl.when(t % 3 == 2)(lambda: piece_on(f))

        t0 = 3 * pieces
        pl.when(t == t0)(hidden_back)

        @pl.when(t == t0 + 1)
        def _():
            lax.fori_loop(0, rows // 2, lambda r, i: (attention_back(r), i)[1], 0)

        @pl.when(t == t0 + 2)
        def _():
            lax.fori_loop(rows // 2, rows, lambda r, i: (attention_back(r), i)[1], 0)
            normed_in().wait()
            put(6 * width, width, tn(nm[...], qkv[:, 0:256]))

        @pl.when(t == t0 + 3)
        def _():
            put(0, width, tn(nm[...], qkv[:, 256:1280]))

        @pl.when(t == t0 + 6)
        def _():
            put(0, width, tn(nm[...], qkv[:, 1280:2304]))

        @pl.when(t == t0 + 8)
        def _():
            for r in range(rows):
                tokens_back(r)
            pltpu.make_async_copy(cot, new_grad, out_sem.at[1]).start()

    live_s[...] = live_in[...]

    def tick(t, carry):
        events(t)
        compute(t)
        pl.when(t < n_chunks)(lambda: half_out(t).start())
        tiny_steps(t, 0, 0, live_s)
        tiny_steps(t, n_chunks, 1, vecs)
        return carry

    lax.fori_loop(0, n_chunks + lags[-1] + 1, tick, 0)

    def last(c, carry):
        half_back(c, sub).wait_send()
        half_back(c, 1 - sub).wait_recv()
        return carry

    lax.fori_loop(0, n_chunks, last, 0)
    pltpu.make_async_copy(dmix, new_block, out_sem.at[0]).wait()
    pltpu.make_async_copy(cot, new_grad, out_sem.at[1]).wait()


def device_sums(mesh, made, weights, vectors):
    picked, cot, dmix, normed, qkv, att, cols, bias, branch, nm, live = made
    w_qkv, w_out, w_up, w_down = weights
    tokens, width = nm.shape
    chosen = bias.shape[1]
    hidden = w_up.shape[1]
    dims = {16: (4, 2, 2), 64: (4, 4, 4)}[mesh.shape["dp"]]
    n_steps = 2 * sum(ROUNDS[n] for n in dims)
    lags = lags_of(n_steps)
    slots = lags[n_steps // 2 + 1] + 1
    chunks = (2 * width * hidden + width * width * 4) // (128 * CHUNK)
    part_rows = CHUNK // 4
    came = max(recv_rows(order, part_rows) for order in ((dims[2], dims[0], dims[1]), (dims[1], dims[0], dims[2])))
    n_tiny = 1 + sum({1: 0, 2: 1, 4: 2}[n] for n in dims)
    n_small = 32 + 8 * (hidden // PIECE)
    vmem, dma = pltpu.VMEM, pltpu.SemaphoreType.DMA
    big = pl.BlockSpec(memory_space=pl.ANY)
    near = pl.BlockSpec(memory_space=vmem)
    return pl.pallas_call(
        functools.partial(sums_kernel, dict(dims=dims, lags=lags, chunks=chunks, small=n_small)),
        in_specs=[big] * 14 + [near] * 6,
        out_specs=[big, near, big, big],
        out_shape=[
            jax.ShapeDtypeStruct((chunks, 2, CHUNK // 2, 128), F32),
            jax.ShapeDtypeStruct((n_small, 128), F32),
            jax.ShapeDtypeStruct((tokens, width), BF16),
            jax.ShapeDtypeStruct((tokens, width), BF16),
        ],
        scratch_shapes=[
            vmem((tokens, width), BF16),
            vmem((width, tokens), BF16),
            vmem((tokens, width), BF16),
            vmem((2, width, PIECE), BF16),
            vmem((2, PIECE, width), BF16),
            vmem((tokens, PIECE), BF16),
            vmem((tokens, PIECE), F32),
            vmem((tokens, PIECE), BF16),
            vmem((tokens, width), F32),
            vmem((tokens, width), F32),
            vmem((tokens, 3 * width), BF16),
            vmem((tokens, width), BF16),
            vmem((tokens, 128), F32),
            vmem((tokens, chosen), BF16),
            vmem((2, chosen, width), F32),
            vmem((tokens, width), BF16),
            vmem((tokens, width), BF16),
            vmem((width, 3 * width), BF16),
            vmem((width, width), BF16),
            vmem((3 * CHUNK, 128), F32),
            vmem((3, CHUNK // 2, 128), F32),
            vmem((slots, CHUNK // 2, 128), F32),
            vmem((slots, 2, came, 128), F32),
            vmem((n_small, 128), F32),
            vmem((8, 128), F32),
            vmem((2, n_tiny, n_small + 8, 128), F32),
            dma((11,)),
            dma((2, 2)),
            dma((2,)),
            dma((2,)),
            dma((3,)),
            dma((3,)),
            dma((slots, 2, n_steps)),
            dma((slots, 2, n_steps)),
            dma((slots, 2)),
            dma((chunks,)),
            dma((chunks,)),
            dma((2, n_tiny)),
            dma((2, n_tiny)),
        ],
        compiler_params=pltpu.CompilerParams(collective_id=0, has_side_effects=True, vmem_limit_bytes=63 * 2**20),
    )(nm, dmix, normed, qkv, att, cols, bias, branch, picked, cot, w_up, w_down, w_qkv, w_out, live, *vectors)


def last_kernel(
    selected, tokens, cot, new_block, new_grad, small, sums,
    block_out, grad_tokens, grad_qkv, grad_out, grad_up, grad_down,
    grad_router, grad_gain_attn, grad_gain_mlp, grad_b_down, grad_b_up, near, in_sems, sems,
):
    step = pl.program_id(0) * pl.num_programs(1) + pl.program_id(1)
    width, hidden = grad_up.shape
    copies = []

    def copy(row, n, dst):
        copies.append((row // GROUP, pltpu.make_async_copy(near.at[pl.ds(row, n)], dst, sems.at[len(copies)])))
        return row + n

    row = 0
    for f in range(0, hidden, PIECE):
        for j in range(0, width, 128):
            row = copy(row, PIECE, grad_down.at[pl.ds(f, PIECE), pl.ds(j, 128)])
        for j in range(f, f + PIECE, 128):
            row = copy(row, width, grad_up.at[:, pl.ds(j, 128)])
    for j in range(0, width, 128):
        row = copy(row, width, grad_out.at[:, pl.ds(j, 128)])
    for j in range(0, 3 * width, 128):
        row = copy(row, width, grad_qkv.at[:, pl.ds(j, 128)])

    groups = sums.shape[0] // GROUP
    fetch = [
        pltpu.make_async_copy(sums.at[pl.ds(g * GROUP, GROUP)], near.at[pl.ds(g * GROUP, GROUP)], in_sems.at[g])
        for g in range(groups)
    ]
    steps = pl.num_programs(0) * pl.num_programs(1)

    @pl.when(step == 0)
    def _():
        for f in fetch:
            f.start()
        for at, out in ((0, grad_router), (8, grad_gain_attn), (16, grad_gain_mlp), (24, grad_b_down)):
            for j in range(width // 128):
                out[j * 128 : (j + 1) * 128] = small[at + j]
        for j in range(hidden // 128):
            grad_b_up[j * 128 : (j + 1) * 128] = small[32 + 8 * (j * 128 // PIECE) + j % (PIECE // 128)]

    for g in range(groups):

        @pl.when(step == jnp.minimum(g, steps - 1))
        def _(g=g):
            fetch[g].wait()
            for at, c in copies:
                if at == g:
                    c.start()

    spots = tokens.shape[1]
    sel = selected[pl.ds(pl.program_id(0), 1)]
    spot = lax.broadcasted_iota(jnp.int32, (spots, sel.shape[1]), 0) + pl.program_id(1) * spots
    hot = jnp.where(spot == sel, 1.0, 0.0)
    hit = jnp.max(hot, axis=-1, keepdims=True) > 0.0
    hot = hot.astype(BF16)
    for old, new, out in ((tokens, new_block, block_out), (cot, new_grad, grad_tokens)):
        fresh = nn(hot, new[...])
        out[0] = jnp.where(hit, fresh, old[0].astype(F32)).astype(BF16)

    @pl.when(step == steps - 1)
    def _():
        for _, c in copies:
            c.wait()


def last(tokens, cotangent, selected, new_block, new_grad, small, sums, hidden):
    rows, spots, width = tokens.shape
    chosen = selected.shape[1]
    cut = 1024
    big = pl.BlockSpec(memory_space=pl.ANY)
    table = pl.BlockSpec((1, cut, width), lambda r, i: (r, i, 0))
    fresh = pl.BlockSpec((chosen, width), lambda r, i: (r, 0))
    vectors = (width, width, width, width, hidden)

    def whole(shape):
        return pl.BlockSpec(shape, lambda r, i: (0,) * len(shape))

    n_copies = hidden // PIECE * (width // 128) + hidden // 128 + 4 * (width // 128)
    return pl.pallas_call(
        last_kernel,
        grid=(rows, spots // cut),
        in_specs=[whole(selected.shape), table, table, fresh, fresh, whole(small.shape), big],
        out_specs=[table, table, big, big, big, big] + [whole((n,)) for n in vectors],
        out_shape=[
            jax.ShapeDtypeStruct(tokens.shape, BF16),
            jax.ShapeDtypeStruct(tokens.shape, BF16),
            jax.ShapeDtypeStruct((width, 3 * width), F32),
            jax.ShapeDtypeStruct((width, width), F32),
            jax.ShapeDtypeStruct((width, hidden), F32),
            jax.ShapeDtypeStruct((hidden, width), F32),
            *(jax.ShapeDtypeStruct((n,), F32) for n in vectors),
        ],
        scratch_shapes=[
            pltpu.VMEM(sums.shape, F32),
            pltpu.SemaphoreType.DMA((sums.shape[0] // GROUP,)),
            pltpu.SemaphoreType.DMA((n_copies,)),
        ],
        compiler_params=pltpu.CompilerParams(vmem_limit_bytes=63 * 2**20),
    )(selected, tokens, cotangent, new_block, new_grad, small, sums)


def body(
    mesh, tokens, doc_lengths, selected, w_router, gain_attn, w_qkv, w_out, gain_mlp, w_up, b_up, w_down, b_down, cotangent
):
    hidden = w_up.shape[1]
    made = first(tokens, doc_lengths, selected, cotangent, w_router, gain_attn, w_qkv, w_out, gain_mlp)
    sums, small, new_block, new_grad = device_sums(
        mesh, made, (w_qkv, w_out, w_up, w_down), (b_up, b_down, w_router, gain_attn, gain_mlp)
    )
    block_out, grad_tokens, grad_qkv, grad_out, grad_up, grad_down, *vectors = last(
        tokens, cotangent, selected, new_block, new_grad, small, sums.reshape(-1, 128), hidden
    )
    grad_router, grad_gain_attn, grad_gain_mlp, grad_b_down, grad_b_up = vectors
    return (
        block_out,
        grad_tokens,
        grad_router,
        grad_gain_attn,
        grad_qkv,
        grad_out,
        grad_gain_mlp,
        grad_up,
        grad_b_up,
        grad_down,
        grad_b_down,
    )


def solution(mesh):
    split, copied = P(("dp", "sub")), P()
    return jax.shard_map(
        functools.partial(body, mesh),
        mesh=mesh,
        in_specs=(split,) * 3 + (copied,) * 9 + (split,),
        out_specs=(split,) * 2 + (copied,) * 9,
        check_vma=False,
    )
```
